256 devices in a mesh: band: 32 (over y, z_hi, core), slab: 8 (over z_lo, x).
Axes of the slice: x: 4, y: 4, z: 8 (z_hi: 4, z_lo: 2; z = z_hi * 2 + z_lo), core: 2. Of those that a mesh axis runs over, the one named last changes fastest.
Arguments:
- orbitals: float32 [32, 160, 160, 160], P('band', 'slab'), may hold values from -6 to 6
Outputs:
- exchange_field: float32 [32, 160, 160, 160], P('band', 'slab')
The draws below stay inside these ranges and needn't reach their ends.
All inputs are finite; a program needn't handle non-finite values.
Results may differ from the reference program's by a relative error of at most 0.0003.
Values sent between devices are 32-bit elements; how exact they have to be, the bound alone decides.
No kernel may reach another device: no remote copies, remote signals or barrier semaphores. Data moves between devices by JAX's collectives and lax.ppermute only.
A program may use at most 128 MiB of HBM per device.

```python
import math
import jax
import jax.numpy as jnp
from jax import lax

NG = 160
STEPS = 2
BANDS = 32


def draw_orbitals(key, part):
    key = jax.random.fold_in(key, 11)
    phase_key, height_key, rough_key = jax.random.split(key, 3)
    bands = jnp.arange(BANDS, dtype=jnp.int32)
    first_y = NG * 12 // 160
    first_x = NG * 3 // 160
    second_y = NG * 14 // 160
    second_x = NG * 3 // 160
    halves = bands // 2
    parity = bands % 2
    wave_y = (halves * (first_y + second_y) + parity * first_y) % NG
    wave_x = (halves * (first_x + second_x) + parity * first_x) % NG
    wave_z = bands * (NG // 4) % NG
    grid = jnp.arange(NG, dtype=jnp.int32)
    along_z = wave_z[:, None, None, None] * grid[None, :, None, None] % NG
    along_y = wave_y[:, None, None, None] * grid[None, None, :, None] % NG
    along_x = wave_x[:, None, None, None] * grid[None, None, None, :] % NG
    index = (along_z + along_y + along_x) % NG
    offsets = jax.random.uniform(phase_key, (BANDS,), jnp.float32) * (2.0 * math.pi)
    angles = index.astype(jnp.float32) * (2.0 * math.pi / NG) + offsets[:, None, None, None]
    shape = (BANDS, NG, NG, NG)
    heights = jax.random.uniform(height_key, (BANDS,), jnp.float32, 3.5, 4.0)
    rough = jnp.clip(jax.random.normal(rough_key, shape, jnp.float32), -6.0, 6.0) * 0.1
    return heights[:, None, None, None] * jnp.cos(angles) + rough


def setup_inputs(seed: int = 0) -> dict:
    seeds = jax.random.split(jax.random.key(seed), 2)
    orbitals = draw_orbitals(jax.random.fold_in(seeds[1], 71), 0)
    return {"orbitals": orbitals}


highest = lax.Precision.HIGHEST


def cas_table(length):
    indices = jnp.arange(length, dtype=jnp.int32)
    product = (indices[:, None] * indices[None, :]) % length
    phases = product.astype(jnp.float32) * (2.0 * math.pi / length)
    return jnp.cos(phases) + jnp.sin(phases)


def wave_square(indices, length):
    return 4.0 * jnp.sin(indices.astype(jnp.float32) * (math.pi / length)) ** 2


def reference(orbitals):
    hartley = cas_table(NG)
    waves = wave_square(jnp.arange(NG, dtype=jnp.int32), NG)
    square = waves[:, None, None] + waves[None, :, None] + waves[None, None, :]
    kernel = jnp.where(square > 0, 1.0 / jnp.where(square > 0, square, 1.0), 0.0)

    def potential(density):
        field = jnp.einsum('xk,zyx->zyk', hartley, density, precision=highest)
        field = jnp.einsum('yk,zyx->zkx', hartley, field, precision=highest)
        field = jnp.einsum('zk,zyx->kyx', hartley, field, precision=highest)
        field = field * kernel
        field = jnp.einsum('zk,zyx->kyx', hartley, field, precision=highest)
        field = jnp.einsum('xk,zyx->zyk', hartley, field, precision=highest)
        field = jnp.einsum('yk,zyx->zkx', hartley, field, precision=highest)
        return field / float(NG ** 3)

    def pair_field(members):
        return potential(members[0] * members[1])

    total = jnp.zeros(orbitals.shape, jnp.float32)
    for offset in range(1, STEPS + 1):
        visiting = jnp.roll(orbitals, offset, axis=0)
        potentials = lax.map(pair_field, (orbitals, visiting))
        total = total + potentials * visiting + jnp.roll(potentials * orbitals, -offset, axis=0)
    return total
```

```python
import functools

import jax
import jax.numpy as jnp
import ml_dtypes
import numpy as np
from jax import lax
from jax.experimental import pallas as pl
from jax.experimental.pallas import tpu as pltpu
from jax.sharding import PartitionSpec as P

NG = 160
SLABS = 8
DEPTH = NG // SLABS
PLANES = 4
CHUNKS = DEPTH // PLANES
WIDE = 256
MODE_TILES = NG * NG // 1024
SEND_TILES = 13
F32 = jnp.float32
BF16 = jnp.bfloat16


def split_table(table):
    high = table.astype(np.float32).astype(ml_dtypes.bfloat16)
    low = (table - high.astype(np.float64)).astype(np.float32).astype(ml_dtypes.bfloat16)
    return high, low


def plane_tiles(plane):
    main = plane[:, :128].reshape(-1, 8, 128)
    rest = np.concatenate([plane[40 * g : 40 * g + 40, 128:] for g in range(4)], axis=1)
    return np.concatenate([main, rest.reshape(-1, 8, 128)])


def widened(plane):
    return np.pad(plane, [(0, 0)] * (plane.ndim - 1) + [(0, WIDE - NG)])


@functools.cache
def tables():
    index = np.arange(NG)
    angle = 2.0 * np.pi * (index[:, None] * index[None, :] % NG) / NG
    hartley = np.cos(angle) + np.sin(angle)
    forward = np.zeros((PLANES, WIDE, WIDE))
    inverse = np.zeros((PLANES, WIDE, WIDE))
    for j in range(PLANES):
        forward[j, :128, :NG] = hartley[:128]
        forward[j, 128 + 32 * j : 160 + 32 * j, :NG] = hartley[128:]
        inverse[j, :NG, :128] = hartley[:, :128]
        inverse[j, :NG, 128 + 32 * j : 160 + 32 * j] = hartley[:, 128:]
    wave = 4.0 * np.sin(np.pi * index / NG) ** 2
    lam = wave[:, None] + wave[None, :]
    ratio = 1.0 / (1.0 + lam / 2 + np.sqrt(lam + lam * lam / 4))
    ratio[0, 0] = 0.0
    scale = ratio / (1.0 - ratio**2) / NG**2
    powers = np.stack([ratio ** (PLANES * k) for k in range(CHUNKS)])
    edge = np.stack([scale * ratio ** (i + 1) for i in range(DEPTH)])
    jump = np.tile(plane_tiles(ratio**DEPTH), (4, 1, 1))
    wrap = np.tile(plane_tiles(1.0 / (1.0 - ratio**NG)), (4, 1, 1))
    spare = [(0, SLABS * SEND_TILES - 4 * MODE_TILES), (0, 0), (0, 0)]
    zero = np.zeros((SLABS, 24, 128))
    for apart in range(SLABS):
        for i in range(DEPTH):
            d = (DEPTH * apart + i - np.arange(DEPTH)) % NG
            zero[apart, i, :DEPTH] = ((NG**2 - 1) / (12 * NG) - d * (NG - d) / (2 * NG)) / NG**2
    as32 = lambda a: a.astype(np.float32)
    return dict(
        forward=np.stack(split_table(forward), axis=1),
        inverse=np.stack(split_table(inverse), axis=1),
        hartley=np.concatenate(split_table(hartley)),
        ratio=as32(widened(ratio)),
        scale=as32(widened(scale)),
        powers=as32(widened(powers)),
        edge=as32(widened(edge)),
        jump=as32(np.pad(jump, spare)),
        wrap=as32(np.pad(wrap, spare)),
        zero=as32(zero),
    )


def split(value):
    high = value.astype(BF16)
    return high, (value - high.astype(F32)).astype(BF16)


def dot(a, b):
    return jnp.dot(a, b, preferred_element_type=F32)


def times_table(value, high_table, low_table):
    high, low = split(value)
    return dot(high, high_table) + dot(low, high_table) + dot(high, low_table)


def table_times(hartley, value):
    high, low = split(value)
    both = dot(hartley, high)
    return both[:NG] + both[NG:] + dot(hartley[:NG], low)


VMEM = pl.BlockSpec(memory_space=pltpu.VMEM)
SMEM = pl.BlockSpec(memory_space=pltpu.SMEM)


def call(kernel, out_shape, in_specs, out_specs, flops=0, moved=0, **kwargs):
    return pl.pallas_call(
        kernel,
        out_shape=out_shape,
        in_specs=in_specs,
        out_specs=out_specs,
        compiler_params=pltpu.CompilerParams(vmem_limit_bytes=40 * 2**20),
        cost_estimate=pl.CostEstimate(flops=flops, bytes_accessed=moved, transcendentals=0),
        **kwargs,
    )


def f32_shape(*shape):
    return jax.ShapeDtypeStruct(shape, F32)


CHUNK = f32_shape(PLANES + 1, NG, 128)


def packed(orbitals, k):
    def kernel(block, out):
        out[:PLANES] = block[0, :, :, :128]
        out[PLANES] = jnp.concatenate([block[0, j, :, 128:] for j in range(PLANES)], axis=1)

    return call(
        kernel,
        CHUNK,
        [pl.BlockSpec((1, PLANES, NG, NG), lambda i: (0, k, 0, 0))],
        pl.BlockSpec((PLANES + 1, NG, 128), lambda i: (0, 0, 0)),
        moved=2 * 10**6,
        grid=(1,),
    )(orbitals)


def to_tiles(plane):
    rest = plane[:, 128:]
    moved = rest[:40]
    for g in range(1, 4):
        moved = moved + pltpu.roll(rest[40 * g : 40 * g + 40], 32 * g, 1)
    return plane[:, :128].reshape(-1, 8, 128), moved.reshape(-1, 8, 128)


def from_tiles(tiles):
    main = jnp.concatenate(tiles[:20], axis=0)
    rest = jnp.concatenate(tiles[20:], axis=0)
    lane = lax.broadcasted_iota(jnp.int32, rest.shape, 1)
    parts = [rest] + [pltpu.roll(rest, 128 - 32 * g, 1) for g in range(1, 4)]
    rest = jnp.concatenate([jnp.where(lane < 32, part, 0.0) for part in parts], axis=0)
    return jnp.concatenate([main, rest], axis=1)


def transformed(k, core, own, swap, vis, state, t):
    first, last = k == 0, k == CHUNKS - 1

    def kernel(*refs):
        core, own, swap, vis, table, hartley, ratio, power = refs[:8]
        refs = refs[8:]
        if not first:
            right0, left0, zero0 = refs[:3]
            refs = refs[3:]
        fields = refs[0]
        visiting, resident, partner = vis[...], own[...], swap[...]
        other = jnp.where(core[0] == 1, visiting, resident)
        densities = (resident * visiting, other * partner)
        h = hartley[...]
        r = ratio[...]
        row = lax.broadcasted_iota(jnp.int32, (8, 128), 0)
        lane = lax.broadcasted_iota(jnp.int32, (8, 128), 1)
        zero = jnp.zeros((8, 128), F32) if first else zero0[...]
        for j in range(PLANES):
            both = jnp.concatenate(
                [jnp.concatenate([d[j], d[PLANES]], axis=1) for d in densities], axis=0
            )
            along_x = times_table(both, table[j, 0], table[j, 1])
            for pair in range(2):
                field = table_times(h, along_x[NG * pair : NG * (pair + 1)])
                fields[pair, j] = field
                here = (row == pair) & (lane == PLANES * k + j)
                zero = jnp.where(here, jnp.broadcast_to(field[:1, :1], (8, 128)), zero)
        rights, lefts = [], []
        for pair in range(2):
            right = fields[pair, 0]
            if not first:
                right = right + r * right0[pair]
            left = fields[pair, PLANES - 1]
            for j in range(1, PLANES):
                right = r * right + fields[pair, j]
                left = r * left + fields[pair, PLANES - 1 - j]
            if not first:
                left = left0[pair] + power[0] * left
            rights.append(right)
            lefts.append(left)
        if not last:
            for pair in range(2):
                refs[1][pair] = rights[pair]
                refs[2][pair] = lefts[pair]
            refs[3][...] = zero
            return
        out = refs[1]
        for number, plane in enumerate(rights + lefts):
            main, rest = to_tiles(plane)
            for i in range(MODE_TILES):
                tile = main[i] if i < 20 else rest[i - 20]
                to, slot = divmod(MODE_TILES * number + i, SEND_TILES)
                out[to, slot] = tile
        for i in range(4 * MODE_TILES, SLABS * SEND_TILES):
            out[i // SEND_TILES, i % SEND_TILES] = jnp.zeros((8, 128), F32)
        for to in range(SLABS):
            out[to, SEND_TILES] = zero

    planes = f32_shape(2, NG, WIDE)
    outs = [f32_shape(2, PLANES, NG, WIDE)]
    outs += [f32_shape(SLABS, SEND_TILES + 1, 8, 128)] if last else [planes, planes, f32_shape(8, 128)]
    whole = lambda a: pl.BlockSpec(a.shape, lambda i: (0,) * len(a.shape))
    operands = [core, own, swap, vis, t["forward"], t["hartley"], t["ratio"], t["powers"]]
    specs = [SMEM] + [whole(a) for a in operands[1:7]]
    specs.append(pl.BlockSpec((1, NG, WIDE), lambda i: (k, 0, 0)))
    if not first:
        operands += state
        specs += [whole(a) for a in state]
    return call(
        kernel,
        outs,
        specs,
        [whole(a) for a in outs],
        flops=2 * 10**9,
        moved=5 * 10**6,
        grid=(1,),
    )(*operands)


def local_part(fields, t):
    def kernel(*refs):
        ratio, scale = refs[:2]
        fields, outs = refs[2 : 2 + CHUNKS], refs[2 + CHUNKS :]
        r, c = ratio[...], scale[...]
        for pair in range(2):
            run = jnp.zeros((NG, WIDE), F32)
            for z in range(DEPTH):
                k, j = divmod(z, PLANES)
                run = r * run + fields[k][pair, j]
                outs[k][pair, j] = run
            run = jnp.zeros((NG, WIDE), F32)
            for z in reversed(range(DEPTH)):
                k, j = divmod(z, PLANES)
                outs[k][pair, j] = c * (outs[k][pair, j] + run)
                run = r * (run + fields[k][pair, j])

    shape = f32_shape(2, PLANES, NG, WIDE)
    return call(
        kernel,
        [shape] * CHUNKS,
        [VMEM] * (2 + CHUNKS),
        [VMEM] * CHUNKS,
        flops=10**7,
        moved=13 * 10**6,
    )(t["ratio"], t["scale"], *fields)


def solved(slab, moments, jump, wrap, t):
    def kernel(slab, moments, jump, wrap, table, out, mean):
        me = slab[0]
        for slot in range(SEND_TILES):
            leftward = me * SEND_TILES + slot >= 2 * MODE_TILES
            place = lambda p: jnp.where(leftward, SLABS - 1 - p, p)
            values = [moments[place(p), slot] for p in range(SLABS)]
            r = jump[slot]
            run = values[0]
            for p in range(1, SLABS):
                run = run * r + values[p]
            run = run * wrap[slot]
            for p in range(SLABS):
                out[place(p), slot] = run
                run = values[p] + r * run
        for pair in range(2):
            total = jnp.zeros((24, 128), F32)
            for p in range(SLABS):
                apart = lax.rem(me - p + SLABS, SLABS)
                total = total + table[apart] * moments[p, SEND_TILES, pair : pair + 1, :]
            mean[pair] = jnp.broadcast_to(jnp.sum(total, axis=1, keepdims=True), (24, 128))

    return call(
        kernel,
        [f32_shape(SLABS, SEND_TILES, 8, 128), f32_shape(2, 24, 128)],
        [SMEM] + [VMEM] * 4,
        [VMEM] * 2,
        flops=10**6,
        moved=10**6,
    )(slab, moments, jump, wrap, t["zero"])


def products(k, core, own, swap, vis, local, coming, mean, t):
    def kernel(core, own, swap, vis, local, coming, mean, left, right, table, hartley, sent, crossed, kept):
        h = hartley[...]
        row = lax.broadcasted_iota(jnp.int32, (NG, WIDE), 0)
        lane = lax.broadcasted_iota(jnp.int32, (NG, WIDE), 1)
        corner = (row == 0) & (lane == 0)
        edges = []
        for number in range(4):
            tiles = []
            for i in range(MODE_TILES):
                tiles.append(coming[divmod(MODE_TILES * number + i, SEND_TILES)])
            edges.append(from_tiles(tiles))
        mains = [[], []]
        rests = [None, None]
        for j in range(PLANES):
            along_y = []
            for pair in range(2):
                field = local[pair, j] + left[j] * edges[pair] + right[PLANES - 1 - j] * edges[2 + pair]
                middle = mean[pair, PLANES * k + j : PLANES * k + j + 1, :1]
                field = jnp.where(corner, jnp.broadcast_to(middle, (NG, WIDE)), field)
                along_y.append(table_times(h, field))
            both = times_table(jnp.concatenate(along_y, axis=0), table[j, 0], table[j, 1])
            for pair in range(2):
                field = both[NG * pair : NG * (pair + 1)]
                mains[pair].append(field[:, :128])
                rest = field[:, 128:]
                rests[pair] = rest if j == 0 else rests[pair] + rest
        second = core[0] == 1
        for j in range(PLANES + 1):
            x, y = (mains[pair][j] if j < PLANES else rests[pair] for pair in range(2))
            resident, partner, visiting = own[j], swap[j], vis[j]
            extra = y * partner
            nothing = jnp.zeros_like(extra)
            sent[j] = x * resident + jnp.where(second, extra, nothing)
            kept[j] = x * visiting + jnp.where(second, nothing, extra)
            crossed[j] = y * jnp.where(second, visiting, resident)

    whole = lambda a: pl.BlockSpec(a.shape, lambda i: (0,) * len(a.shape))
    operands = [core, own, swap, vis, local, coming, mean, t["edge"], t["edge"], t["inverse"], t["hartley"]]
    specs = [SMEM] + [whole(a) for a in operands[1:7]]
    specs.append(pl.BlockSpec((PLANES, NG, WIDE), lambda i: (k, 0, 0)))
    specs.append(pl.BlockSpec((PLANES, NG, WIDE), lambda i: (CHUNKS - 1 - k, 0, 0)))
    specs += [whole(a) for a in operands[9:]]
    return call(
        kernel,
        [CHUNK] * 3,
        specs,
        [whole(CHUNK)] * 3,
        flops=2 * 10**9,
        moved=6 * 10**6,
        grid=(1,),
    )(*operands)


def finished(k, kept, crossed, returned, result):
    def kernel(kept, crossed, returned, *refs):
        out = refs[-1]
        total = kept[...] + crossed[...] + returned[...]
        out[0, :, :, :128] = total[:PLANES]
        rest = total[PLANES]
        for j in range(PLANES):
            moved = rest if j == 0 else pltpu.roll(rest, 128 - 32 * j, 1)
            out[0, j, :, 128:] = moved[:, :32]

    operands = [kept, crossed, returned]
    specs = [pl.BlockSpec(CHUNK.shape, lambda i: (0, 0, 0))] * 3
    aliases = {}
    if result is not None:
        operands.append(result)
        specs.append(pl.BlockSpec(memory_space=pl.ANY))
        aliases = {3: 0}
    return call(
        kernel,
        f32_shape(1, DEPTH, NG, NG),
        specs,
        pl.BlockSpec((1, PLANES, NG, NG), lambda i: (0, k, 0, 0)),
        moved=2 * 10**6,
        grid=(1,),
        input_output_aliases=aliases,
    )(*operands)


def shards(orbitals):
    t = {name: jnp.asarray(table) for name, table in tables().items()}
    bands = lax.axis_size("band")
    core = lax.rem(lax.axis_index("band"), 2).astype(jnp.int32).reshape(1)
    slab = lax.axis_index("slab").astype(jnp.int32)
    outward = [(g, (g - 2) % bands if g % 2 == 0 else (g + 2) % bands) for g in range(bands)]
    homeward = [(b, a) for a, b in outward]
    across = [(g, g ^ 1) for g in range(bands)]
    jump = lax.dynamic_slice_in_dim(t["jump"], slab * SEND_TILES, SEND_TILES)
    wrap = lax.dynamic_slice_in_dim(t["wrap"], slab * SEND_TILES, SEND_TILES)

    own = [packed(orbitals, k) for k in range(CHUNKS)]
    vis = [lax.ppermute(chunk, "band", outward) for chunk in own]
    swap = [lax.ppermute(chunk, "band", across) for chunk in own]

    fields, state = [], None
    for k in range(CHUNKS):
        field, *state = transformed(k, core, own[k], swap[k], vis[k], state, t)
        fields.append(field)
    shape = state[0].shape
    moments = state[0].reshape(-1, 128)
    moments = lax.all_to_all(moments, "slab", 0, 0, tiled=True).reshape(shape)
    local = local_part(fields, t)
    coming, mean = solved(slab.reshape(1), moments, jump, wrap, t)
    shape = coming.shape
    coming = lax.all_to_all(coming.reshape(-1, 128), "slab", 0, 0, tiled=True).reshape(shape)

    kept, crossed, returned = [], [], []
    for k in range(CHUNKS):
        sent, partner, here = products(k, core, own[k], swap[k], vis[k], local[k], coming, mean, t)
        returned.append(lax.ppermute(sent, "band", homeward))
        crossed.append(lax.ppermute(partner, "band", across))
        kept.append(here)
    result = None
    for k in range(CHUNKS):
        result = finished(k, kept[k], crossed[k], returned[k], result)
    return result


def solution(mesh):
    spec = P("band", "slab", None, None)
    return jax.shard_map(shards, mesh=mesh, in_specs=(spec,), out_specs=spec, check_vma=False)
```

```python
import functools

import jax
import jax.numpy as jnp
import ml_dtypes
import numpy as np
from jax import lax
from jax.experimental import pallas as pl
from jax.experimental.pallas import tpu as pltpu
from jax.sharding import PartitionSpec as P

NG = 160
SLABS = 8
DEPTH = NG // SLABS
PLANES = 4
CHUNKS = DEPTH // PLANES
WIDE = 256
MODE_TILES = NG * NG // 1024
SEND_TILES = 13
F32 = jnp.float32
BF16 = jnp.bfloat16


def split_table(table):
    high = table.astype(np.float32).astype(ml_dtypes.bfloat16)
    low = (table - high.astype(np.float64)).astype(np.float32).astype(ml_dtypes.bfloat16)
    return high, low


def stacked(table, axis):
    high, low = split_table(table)
    return np.concatenate([high, high, low] if axis == 0 else [high, low, high], axis=axis)


def plane_tiles(plane):
    main = plane[:, :128].reshape(-1, 8, 128)
    rest = np.concatenate([plane[40 * g : 40 * g + 40, 128:] for g in range(4)], axis=1)
    return np.concatenate([main, rest.reshape(-1, 8, 128)])


def widened(plane):
    return np.pad(plane, [(0, 0)] * (plane.ndim - 1) + [(0, WIDE - NG)])


@functools.cache
def tables():
    index = np.arange(NG)
    angle = 2.0 * np.pi * (index[:, None] * index[None, :] % NG) / NG
    hartley = np.cos(angle) + np.sin(angle)
    forward = np.zeros((WIDE, WIDE))
    forward[:128, :NG] = hartley[:128]
    forward[128:, :NG] = np.tile(hartley[128:], (PLANES, 1))
    inverse = np.zeros((WIDE, WIDE))
    inverse[:NG, :128] = hartley[:, :128]
    inverse[:NG, 128:] = np.tile(hartley[:, 128:], (1, PLANES))
    wave = 4.0 * np.sin(np.pi * index / NG) ** 2
    lam = wave[:, None] + wave[None, :]
    ratio = 1.0 / (1.0 + lam / 2 + np.sqrt(lam + lam * lam / 4))
    ratio[0, 0] = 0.0
    scale = ratio / (1.0 - ratio**2) / NG**2
    powers = np.stack([ratio ** (PLANES * k) for k in range(CHUNKS)])
    edge = np.stack([scale * ratio ** (i + 1) for i in range(DEPTH)])
    jump = np.tile(plane_tiles(ratio**DEPTH), (4, 1, 1))
    wrap = np.tile(plane_tiles(1.0 / (1.0 - ratio**NG)), (4, 1, 1))
    spare = [(0, SLABS * SEND_TILES - 4 * MODE_TILES), (0, 0), (0, 0)]
    zero = np.zeros((SLABS, 24, 128))
    for apart in range(SLABS):
        for i in range(DEPTH):
            d = (DEPTH * apart + i - np.arange(DEPTH)) % NG
            zero[apart, i, :DEPTH] = ((NG**2 - 1) / (12 * NG) - d * (NG - d) / (2 * NG)) / NG**2
    as32 = lambda a: a.astype(np.float32)
    return dict(
        forward=stacked(forward, 0),
        inverse=stacked(inverse, 0),
        hartley=stacked(hartley, 1),
        ratio=as32(widened(ratio)),
        scale=as32(widened(scale)),
        powers=as32(widened(powers)),
        edge=as32(widened(edge)),
        jump=as32(np.pad(jump, spare)),
        wrap=as32(np.pad(wrap, spare)),
        zero=as32(zero),
    )


def split(value):
    high = value.astype(BF16)
    return high, (value - high.astype(F32)).astype(BF16)


def dot(a, b):
    return jnp.dot(a, b, preferred_element_type=F32)


def times_table(value, table):
    high, low = split(value)
    return dot(jnp.concatenate([high, low, high], axis=1), table)


def table_times(table, value):
    high, low = split(value)
    return dot(table, jnp.concatenate([high, high, low], axis=0))


VMEM = pl.BlockSpec(memory_space=pltpu.VMEM)
SMEM = pl.BlockSpec(memory_space=pltpu.SMEM)
HBM = pl.BlockSpec(memory_space=pltpu.HBM)
GROUPS = (2, 2, 1)
FIRST = tuple(sum(GROUPS[:g]) for g in range(len(GROUPS)))


def call(kernel, name, operands, outs, in_specs=None, out_specs=VMEM, limit=14, **kwargs):
    if in_specs is None:
        in_specs = [VMEM] * len(operands)
    return pl.pallas_call(
        kernel,
        name=name,
        out_shape=outs,
        in_specs=in_specs,
        out_specs=jax.tree.map(lambda a: out_specs, outs),
        compiler_params=pltpu.CompilerParams(vmem_limit_bytes=limit * 2**20),
        cost_estimate=pl.CostEstimate(flops=1, bytes_accessed=1, transcendentals=0),
        **kwargs,
    )(*operands)


def at(g, arrays):
    place = pltpu.VMEM if g == len(GROUPS) - 1 else pltpu.HBM
    return [pltpu.with_memory_space_constraint(a, place) for a in arrays]


def kept_close(arrays):
    return [pltpu.with_memory_space_constraint(a, pltpu.VMEM) for a in arrays]


def space(g):
    return pltpu.VMEM


def f32_shape(*shape):
    return jax.ShapeDtypeStruct(shape, F32)


def group_shape(g):
    return space(g)((GROUPS[g] * (PLANES + 1), NG, 128), F32)


def packed(orbitals, g):
    count = GROUPS[g] * PLANES

    def kernel(orbitals, out, block, arrived):
        copy = pltpu.make_async_copy(
            orbitals.at[0, pl.ds(FIRST[g] * PLANES, count)], block, arrived
        )
        copy.start()
        copy.wait()
        for c in range(GROUPS[g]):
            base = c * (PLANES + 1)
            planes = range(c * PLANES, (c + 1) * PLANES)
            for j, z in enumerate(planes):
                out[base + j] = block[z, :, :128]
            out[base + PLANES] = jnp.concatenate([block[z, :, 128:] for z in planes], axis=1)

    return call(
        kernel,
        f"pack_{g}",
        [pltpu.with_memory_space_constraint(orbitals, pltpu.HBM)],
        group_shape(g),
        [HBM],
        scratch_shapes=[pltpu.VMEM((count, NG, NG), F32), pltpu.SemaphoreType.DMA],
    )


def strip():
    return lax.broadcasted_iota(jnp.int32, (NG, 128), 1) // (128 // PLANES)


def to_tiles(plane):
    rest = plane[:, 128:]
    moved = rest[:40]
    for g in range(1, 4):
        moved = moved + pltpu.roll(rest[40 * g : 40 * g + 40], 32 * g, 1)
    return plane[:, :128].reshape(-1, 8, 128), moved.reshape(-1, 8, 128)


def from_tiles(tiles):
    main = jnp.concatenate(tiles[:20], axis=0)
    rest = jnp.concatenate(tiles[20:], axis=0)
    lane = lax.broadcasted_iota(jnp.int32, rest.shape, 1)
    parts = [rest] + [pltpu.roll(rest, 128 - 32 * g, 1) for g in range(1, 4)]
    rest = jnp.concatenate([jnp.where(lane < 32, part, 0.0) for part in parts], axis=0)
    return jnp.concatenate([main, rest], axis=1)


def transformed(g, core, own, swap, vis, state, t):
    first, last = g == 0, g == len(GROUPS) - 1

    def kernel(*refs):
        core, own, swap, vis, table, hartley, ratio, powers = refs[:8]
        refs = refs[8:]
        if not first:
            right0, left0, zero0 = refs[:3]
            refs = refs[3:]
        fields, *results = refs
        second = core[0] == 1
        h, r, x_table, owner = hartley[...], ratio[...], table[...], strip()
        row = lax.broadcasted_iota(jnp.int32, (8, 128), 0)
        lane = lax.broadcasted_iota(jnp.int32, (8, 128), 1)
        means = jnp.zeros((8, 128), F32) if first else zero0[...]
        rights = [None if first else right0[pair] for pair in range(2)]
        lefts = [None if first else left0[pair] for pair in range(2)]
        for c in range(GROUPS[g]):
            start = c * (PLANES + 1)
            densities = []
            for p in range(start, start + PLANES + 1):
                other = jnp.where(second, vis[p], own[p])
                densities.append((own[p] * vis[p], other * swap[p]))
            for j in range(PLANES):
                wide = [
                    jnp.concatenate([densities[j][pair], jnp.where(owner == j, densities[PLANES][pair], 0.0)], axis=1)
                    for pair in range(2)
                ]
                along_x = times_table(jnp.concatenate(wide, axis=0), x_table)
                z = PLANES * c + j
                for pair in range(2):
                    field = table_times(h, along_x[NG * pair : NG * (pair + 1)])
                    fields[pair, z] = field
                    rights[pair] = field if rights[pair] is None else r * rights[pair] + field
                    here = (row == pair) & (lane == PLANES * FIRST[g] + z)
                    means = jnp.where(here, jnp.broadcast_to(field[:1, :1], (8, 128)), means)
            for pair in range(2):
                back = fields[pair, PLANES * c + PLANES - 1]
                for j in reversed(range(PLANES - 1)):
                    back = r * back + fields[pair, PLANES * c + j]
                lefts[pair] = back if lefts[pair] is None else lefts[pair] + powers[FIRST[g] + c] * back
        if not last:
            right, left, zero = results
            for pair in range(2):
                right[pair] = rights[pair]
                left[pair] = lefts[pair]
            zero[...] = means
            return
        (out,) = results
        for number, plane in enumerate(rights + lefts):
            main, rest = to_tiles(plane)
            for i in range(MODE_TILES):
                tile = main[i] if i < 20 else rest[i - 20]
                to, slot = divmod(MODE_TILES * number + i, SEND_TILES)
                out[to, slot] = tile
        for i in range(4 * MODE_TILES, SLABS * SEND_TILES):
            out[i // SEND_TILES, i % SEND_TILES] = jnp.zeros((8, 128), F32)
        for to in range(SLABS):
            out[to, SEND_TILES] = means

    outs = [space(g)((2, GROUPS[g] * PLANES, NG, WIDE), F32)]
    if last:
        outs += [f32_shape(SLABS, SEND_TILES + 1, 8, 128)]
    else:
        outs += [space(g + 1)((2, NG, WIDE), F32)] * 2 + [f32_shape(8, 128)]
    operands = [core, *kept_close([own]), *at(g, [swap, vis])]
    operands += kept_close([t["forward"], t["hartley"], t["ratio"], t["powers"]])
    if not first:
        operands += [*kept_close(state[:2]), state[2]]
    field, *state = call(
        kernel, f"forward_{g}", operands, outs, [SMEM] + [VMEM] * (len(operands) - 1)
    )
    return field, (state[0] if last else state)


def solved(slab, moments, t):
    def kernel(slab, moments, jumps, wraps, table, out, mean, jump, wrap, arrived):
        me = slab[0]
        mine = pl.ds(me * SEND_TILES, SEND_TILES)
        copies = [
            pltpu.make_async_copy(jumps.at[mine], jump, arrived.at[0]),
            pltpu.make_async_copy(wraps.at[mine], wrap, arrived.at[1]),
        ]
        for copy in copies:
            copy.start()
        for pair in range(2):
            total = jnp.zeros((24, 128), F32)
            for p in range(SLABS):
                apart = lax.rem(me - p + SLABS, SLABS)
                total = total + table[apart] * moments[p, SEND_TILES, pair : pair + 1, :]
            mean[pair] = jnp.broadcast_to(jnp.sum(total, axis=1, keepdims=True), (24, 128))
        for copy in copies:
            copy.wait()
        for slot in range(SEND_TILES):
            leftward = me * SEND_TILES + slot >= 2 * MODE_TILES
            place = lambda p: jnp.where(leftward, SLABS - 1 - p, p)
            values = [moments[place(p), slot] for p in range(SLABS)]
            r = jump[slot]
            run = values[0]
            for p in range(1, SLABS):
                run = run * r + values[p]
            run = run * wrap[slot]
            for p in range(SLABS):
                out[place(p), slot] = run
                run = values[p] + r * run

    tables = [pltpu.with_memory_space_constraint(t[name], pltpu.HBM) for name in ("jump", "wrap")]
    return call(
        kernel,
        "solve",
        [slab, moments, *tables, t["zero"]],
        [f32_shape(SLABS, SEND_TILES, 8, 128), f32_shape(2, 24, 128)],
        [SMEM, VMEM, HBM, HBM, VMEM],
        scratch_shapes=[pltpu.VMEM((SEND_TILES, 8, 128), F32)] * 2 + [pltpu.SemaphoreType.DMA((2,))],
    )


def products(g, core, own, swap, vis, field, before, coming, mean, state, t):
    first, whole = state is None, before is not None

    def kernel(core, own, swap, vis, fields, mean, edge, ratio, scale, table, hartley, *refs):
        if whole:
            before = refs[0]
            refs = refs[1:]
        if first:
            tiles = [[refs[0][divmod(MODE_TILES * n + i, SEND_TILES)] for i in range(MODE_TILES)] for n in range(4)]
            edges = [from_tiles(list_) for list_ in tiles]
            refs = refs[1:]
        else:
            edges = [refs[n // 2][n % 2] for n in range(4)]
            refs = refs[2:]
        sent, crossed, kept, right, left = refs
        rights, lefts = edges[:2], edges[2:]
        second = core[0] == 1
        h, r, c, x_table, owner = hartley[...], ratio[...], scale[...], table[...], strip()
        row = lax.broadcasted_iota(jnp.int32, (NG, WIDE), 0)
        lane = lax.broadcasted_iota(jnp.int32, (NG, WIDE), 1)
        corner = (row == 0) & (lane == 0)
        count = GROUPS[g] * PLANES
        sums = [[], []]
        for pair in range(2):
            run = before[pair] if whole else None
            for z in range(count):
                run = fields[pair, z] if run is None else r * run + fields[pair, z]
                sums[pair].append(run)
        for k in reversed(range(GROUPS[g])):
            start = k * (PLANES + 1)
            rests = [None, None]

            def share(p, x, y):
                resident, partner, visiting = own[p], swap[p], vis[p]
                extra = y * partner
                sent[p] = x * resident + jnp.where(second, extra, 0.0)
                kept[p] = x * visiting + jnp.where(second, 0.0, extra)
                crossed[p] = y * jnp.where(second, visiting, resident)

            for j in reversed(range(PLANES)):
                z = PLANES * k + j
                along_y = []
                for pair in range(2):
                    run = r * lefts[pair]
                    value = c * (sums[pair][z] + run) + edge[z] * rights[pair]
                    lefts[pair] = run + fields[pair, z]
                    middle = mean[pair, PLANES * FIRST[g] + z : PLANES * FIRST[g] + z + 1, :1]
                    value = jnp.where(corner, jnp.broadcast_to(middle, (NG, WIDE)), value)
                    along_y.append(table_times(h, value))
                both = times_table(jnp.concatenate(along_y, axis=0), x_table)
                parts = [both[:NG], both[NG:]]
                for pair in range(2):
                    rest = parts[pair][:, 128:]
                    rests[pair] = rest if rests[pair] is None else jnp.where(owner == j, rest, rests[pair])
                share(start + j, parts[0][:, :128], parts[1][:, :128])
            share(start + PLANES, *rests)
        for pair in range(2):
            right[pair] = rights[pair]
            left[pair] = lefts[pair]

    count = GROUPS[g] * PLANES
    edge = t["edge"][PLANES * FIRST[g] : PLANES * FIRST[g] + count]
    operands = [core, *kept_close([own]), *at(g, [swap, vis]), *kept_close([field]), mean]
    operands += kept_close([edge, t["ratio"], t["scale"], t["inverse"], t["hartley"]])
    if whole:
        operands += kept_close([before])
    operands += [coming] if first else kept_close(state)
    planes = space(g)((2, NG, WIDE), F32)
    sent, crossed, kept, *state = call(
        kernel,
        f"products_{g}",
        operands,
        [group_shape(g)] * 3 + [planes] * 2,
        [SMEM] + [VMEM] * (len(operands) - 1),
    )
    return sent, crossed, kept, state


def finished(g, kept, crossed, returned, result):
    def kernel(kept, crossed, returned, *refs):
        out = refs[-1]
        total = kept[...] + crossed[...] + returned[...]
        out[0, :, :, :128] = total[:PLANES]
        rest = total[PLANES]
        for j in range(PLANES):
            moved = rest if j == 0 else pltpu.roll(rest, 128 - 32 * j, 1)
            out[0, j, :, 128:] = moved[:, :32]

    block = pl.BlockSpec((PLANES + 1, NG, 128), lambda i: (i, 0, 0))
    operands = [kept, crossed, returned]
    specs = [block] * 3
    aliases = {}
    if result is not None:
        operands.append(result)
        specs.append(HBM)
        aliases = {3: 0}
    return call(
        kernel,
        f"finish_{g}",
        operands,
        pltpu.HBM((1, DEPTH, NG, NG), F32),
        specs,
        pl.BlockSpec((1, PLANES, NG, NG), lambda i: (0, FIRST[g] + i, 0, 0)),
        grid=(GROUPS[g],),
        input_output_aliases=aliases,
    )


def exchanged(array):
    flat = array.reshape(-1, 128)
    return lax.all_to_all(flat, "slab", 0, 0, tiled=True).reshape(array.shape)


def moved(name, array, pairs):
    with jax.named_scope(name):
        return lax.ppermute(array, "band", pairs)


def shards(orbitals):
    t = {name: jnp.asarray(table) for name, table in tables().items()}
    bands = lax.axis_size("band")
    core = lax.rem(lax.axis_index("band"), 2).astype(jnp.int32).reshape(1)
    slab = lax.axis_index("slab").astype(jnp.int32).reshape(1)
    outward = [(g, (g - 2) % bands if g % 2 == 0 else (g + 2) % bands) for g in range(bands)]
    homeward = [(b, a) for a, b in outward]
    across = [(g, g ^ 1) for g in range(bands)]

    groups = range(len(GROUPS))
    own = [packed(orbitals, g) for g in groups]
    vis = [moved(f"visit_{g}", own[g], outward) for g in groups]
    swap = [moved(f"swap_{g}", own[g], across) for g in groups]

    fields, befores, state = [], [], None
    for g in groups:
        befores.append(state and state[0])
        field, state = transformed(g, core, own[g], swap[g], vis[g], state, t)
        fields.append(field)
    state, slab, core = lax.optimization_barrier((state, slab, core))
    coming, mean = solved(slab, exchanged(state), t)
    coming = exchanged(coming)

    state, parts = None, []
    for g in reversed(groups):
        if len(parts) == 2:
            number, kept, crossed, returned = parts[0]
            crossed, returned, *state = lax.optimization_barrier((crossed, returned, *state))
            parts[0] = (number, kept, crossed, returned)
        sent, partner, kept, state = products(
            g, core, own[g], swap[g], vis[g], fields[g], befores[g], coming, mean, state, t
        )
        returned = moved(f"return_{g}", sent, homeward)
        crossed = moved(f"cross_{g}", partner, across)
        parts.append((g, kept, crossed, returned))
    result = None
    for part in parts:
        result = finished(*part, result)
    return result


def solution(mesh):
    spec = P("band", "slab", None, None)
    return jax.shard_map(shards, mesh=mesh, in_specs=(spec,), out_specs=spec, check_vma=False)
```

```python
import functools

import jax
import jax.numpy as jnp
import ml_dtypes
import numpy as np
from jax import lax
from jax.experimental import pallas as pl
from jax.experimental.pallas import tpu as pltpu
from jax.sharding import PartitionSpec as P

NG = 160
SLABS = 8
DEPTH = NG // SLABS
PLANES = 4
CHUNKS = DEPTH // PLANES
WIDE = 256
MODE_TILES = NG * NG // 1024
SEND_TILES = 13
F32 = jnp.float32
BF16 = jnp.bfloat16


def split_table(table):
    high = table.astype(np.float32).astype(ml_dtypes.bfloat16)
    low = (table - high.astype(np.float64)).astype(np.float32).astype(ml_dtypes.bfloat16)
    return high, low


def stacked(table, axis):
    high, low = split_table(table)
    return np.concatenate([high, high, low] if axis == 0 else [high, low, high], axis=axis)


def plane_tiles(plane):
    main = plane[:, :128].reshape(-1, 8, 128)
    rest = np.concatenate([plane[40 * g : 40 * g + 40, 128:] for g in range(4)], axis=1)
    return np.concatenate([main, rest.reshape(-1, 8, 128)])


def widened(plane):
    return np.pad(plane, [(0, 0)] * (plane.ndim - 1) + [(0, WIDE - NG)])


@functools.cache
def tables():
    index = np.arange(NG)
    angle = 2.0 * np.pi * (index[:, None] * index[None, :] % NG) / NG
    hartley = np.cos(angle) + np.sin(angle)
    forward = np.zeros((WIDE, WIDE))
    forward[:128, :NG] = hartley[:128]
    forward[128:, :NG] = np.tile(hartley[128:], (PLANES, 1))
    inverse = np.zeros((WIDE, WIDE))
    inverse[:NG, :128] = hartley[:, :128]
    inverse[:NG, 128:] = np.tile(hartley[:, 128:], (1, PLANES))
    wave = 4.0 * np.sin(np.pi * index / NG) ** 2
    lam = wave[:, None] + wave[None, :]
    ratio = 1.0 / (1.0 + lam / 2 + np.sqrt(lam + lam * lam / 4))
    ratio[0, 0] = 0.0
    scale = ratio / (1.0 - ratio**2) / NG**2
    powers = np.stack([ratio ** (PLANES * k) for k in range(CHUNKS)])
    edge = np.stack([scale * ratio ** (i + 1) for i in range(DEPTH)])
    jump = np.tile(plane_tiles(ratio**DEPTH), (4, 1, 1))
    wrap = np.tile(plane_tiles(1.0 / (1.0 - ratio**NG)), (4, 1, 1))
    spare = [(0, SLABS * SEND_TILES - 4 * MODE_TILES), (0, 0), (0, 0)]
    zero = np.zeros((SLABS, 24, 128))
    for apart in range(SLABS):
        for i in range(DEPTH):
            d = (DEPTH * apart + i - np.arange(DEPTH)) % NG
            zero[apart, i, :DEPTH] = ((NG**2 - 1) / (12 * NG) - d * (NG - d) / (2 * NG)) / NG**2
    as32 = lambda a: a.astype(np.float32)
    return dict(
        forward=stacked(forward, 0),
        inverse=stacked(inverse, 0),
        hartley=stacked(hartley, 1),
        ratio=as32(widened(ratio)),
        scale=as32(widened(scale)),
        powers=as32(widened(powers)),
        edge=as32(widened(edge)),
        jump=as32(np.pad(jump, spare)),
        wrap=as32(np.pad(wrap, spare)),
        zero=as32(zero),
    )


def split(value):
    high = value.astype(BF16)
    return high, (value - high.astype(F32)).astype(BF16)


def dot(a, b):
    return jnp.dot(a, b, preferred_element_type=F32)


def times_table(value, table):
    high, low = split(value)
    return dot(jnp.concatenate([high, low, high], axis=1), table)


def table_times(table, value):
    high, low = split(value)
    return dot(table, jnp.concatenate([high, high, low], axis=0))


VMEM = pl.BlockSpec(memory_space=pltpu.VMEM)
SMEM = pl.BlockSpec(memory_space=pltpu.SMEM)
HBM = pl.BlockSpec(memory_space=pltpu.HBM)
GROUPS = (2, 2, 1)
FIRST = tuple(sum(GROUPS[:g]) for g in range(len(GROUPS)))


def call(kernel, name, operands, outs, in_specs=None, out_specs=VMEM, limit=14, **kwargs):
    if in_specs is None:
        in_specs = [VMEM] * len(operands)
    return pl.pallas_call(
        kernel,
        name=name,
        out_shape=outs,
        in_specs=in_specs,
        out_specs=jax.tree.map(lambda a: out_specs, outs),
        compiler_params=pltpu.CompilerParams(vmem_limit_bytes=limit * 2**20),
        cost_estimate=pl.CostEstimate(flops=1, bytes_accessed=1, transcendentals=0),
        **kwargs,
    )(*operands)


def at(g, arrays):
    place = pltpu.VMEM if g == len(GROUPS) - 1 else pltpu.HBM
    return [pltpu.with_memory_space_constraint(a, place) for a in arrays]


def kept_close(arrays):
    return [pltpu.with_memory_space_constraint(a, pltpu.VMEM) for a in arrays]


def space(g):
    return pltpu.VMEM


def f32_shape(*shape):
    return jax.ShapeDtypeStruct(shape, F32)


def group_shape(g):
    return space(g)((GROUPS[g] * (PLANES + 1), NG, 128), F32)


def own_shape(g):
    return group_shape(g) if g == 2 else pltpu.HBM((GROUPS[g] * (PLANES + 1), NG, 128), F32)


def packed(orbitals, g):
    count = GROUPS[g]
    close = g == len(GROUPS) - 1

    def kernel(orbitals, out, block, *refs):
        ready, (arrived, gone) = (out, refs) if close else (refs[0], refs[1:])
        comes, goes = [], []
        for c in range(count):
            there = pl.ds((FIRST[g] + c) * PLANES, PLANES)
            here = pl.ds(c * PLANES, PLANES)
            comes.append(pltpu.make_async_copy(orbitals.at[0, there], block.at[here], arrived.at[c]))
            comes[c].start()
        for c in range(count):
            comes[c].wait()
            base = c * (PLANES + 1)
            planes = range(c * PLANES, (c + 1) * PLANES)
            for j, z in enumerate(planes):
                ready[base + j] = block[z, :, :128]
            ready[base + PLANES] = jnp.concatenate([block[z, :, 128:] for z in planes], axis=1)
            if not close:
                part = pl.ds(base, PLANES + 1)
                goes.append(pltpu.make_async_copy(ready.at[part], out.at[part], gone.at[c]))
                goes[c].start()
        for copy in goes:
            copy.wait()

    scratch = [pltpu.VMEM((count * PLANES, NG, NG), F32)]
    if not close:
        scratch.append(pltpu.VMEM(group_shape(g).shape, F32))
    return call(
        kernel,
        f"pack_{g}",
        [pltpu.with_memory_space_constraint(orbitals, pltpu.HBM)],
        own_shape(g),
        [HBM],
        VMEM if close else HBM,
        scratch_shapes=scratch + [pltpu.SemaphoreType.DMA((count,))] * 2,
    )


def strip():
    return lax.broadcasted_iota(jnp.int32, (NG, 128), 1) // (128 // PLANES)


def to_tiles(plane):
    rest = plane[:, 128:]
    moved = rest[:40]
    for g in range(1, 4):
        moved = moved + pltpu.roll(rest[40 * g : 40 * g + 40], 32 * g, 1)
    return plane[:, :128].reshape(-1, 8, 128), moved.reshape(-1, 8, 128)


def from_tiles(tiles):
    main = jnp.concatenate(tiles[:20], axis=0)
    rest = jnp.concatenate(tiles[20:], axis=0)
    lane = lax.broadcasted_iota(jnp.int32, rest.shape, 1)
    parts = [rest] + [pltpu.roll(rest, 128 - 32 * g, 1) for g in range(1, 4)]
    rest = jnp.concatenate([jnp.where(lane < 32, part, 0.0) for part in parts], axis=0)
    return jnp.concatenate([main, rest], axis=1)


def transformed(g, core, own, swap, vis, state, t):
    first, last = g == 0, g == len(GROUPS) - 1

    def kernel(*refs):
        core, own, swap, vis, table, hartley, ratio, powers = refs[:8]
        refs = refs[8:]
        if not first:
            right0, left0, zero0 = refs[:3]
            refs = refs[3:]
        fields, *results = refs
        second = core[0] == 1
        h, r, x_table, owner = hartley[...], ratio[...], table[...], strip()
        row = lax.broadcasted_iota(jnp.int32, (8, 128), 0)
        lane = lax.broadcasted_iota(jnp.int32, (8, 128), 1)
        means = jnp.zeros((8, 128), F32) if first else zero0[...]
        rights = [None if first else right0[pair] for pair in range(2)]
        lefts = [None if first else left0[pair] for pair in range(2)]
        for c in range(GROUPS[g]):
            start = c * (PLANES + 1)
            densities = []
            for p in range(start, start + PLANES + 1):
                other = jnp.where(second, vis[p], own[p])
                densities.append((own[p] * vis[p], other * swap[p]))
            for j in range(PLANES):
                wide = [
                    jnp.concatenate([densities[j][pair], jnp.where(owner == j, densities[PLANES][pair], 0.0)], axis=1)
                    for pair in range(2)
                ]
                along_x = times_table(jnp.concatenate(wide, axis=0), x_table)
                z = PLANES * c + j
                for pair in range(2):
                    field = table_times(h, along_x[NG * pair : NG * (pair + 1)])
                    fields[pair, z] = field
                    rights[pair] = field if rights[pair] is None else r * rights[pair] + field
                    here = (row == pair) & (lane == PLANES * FIRST[g] + z)
                    means = jnp.where(here, jnp.broadcast_to(field[:1, :1], (8, 128)), means)
            for pair in range(2):
                back = fields[pair, PLANES * c + PLANES - 1]
                for j in reversed(range(PLANES - 1)):
                    back = r * back + fields[pair, PLANES * c + j]
                lefts[pair] = back if lefts[pair] is None else lefts[pair] + powers[FIRST[g] + c] * back
        if not last:
            right, left, zero = results
            for pair in range(2):
                right[pair] = rights[pair]
                left[pair] = lefts[pair]
            zero[...] = means
            return
        (out,) = results
        for number, plane in enumerate(rights + lefts):
            main, rest = to_tiles(plane)
            for i in range(MODE_TILES):
                tile = main[i] if i < 20 else rest[i - 20]
                to, slot = divmod(MODE_TILES * number + i, SEND_TILES)
                out[to, slot] = tile
        for i in range(4 * MODE_TILES, SLABS * SEND_TILES):
            out[i // SEND_TILES, i % SEND_TILES] = jnp.zeros((8, 128), F32)
        for to in range(SLABS):
            out[to, SEND_TILES] = means

    outs = [space(g)((2, GROUPS[g] * PLANES, NG, WIDE), F32)]
    if last:
        outs += [f32_shape(SLABS, SEND_TILES + 1, 8, 128)]
    else:
        outs += [space(g + 1)((2, NG, WIDE), F32)] * 2 + [f32_shape(8, 128)]
    operands = [core, *at(g, [own]), *at(g, [swap, vis])]
    operands += kept_close([t["forward"], t["hartley"], t["ratio"], t["powers"]])
    if not first:
        operands += [*kept_close(state[:2]), state[2]]
    field, *state = call(
        kernel, f"forward_{g}", operands, outs, [SMEM] + [VMEM] * (len(operands) - 1)
    )
    return field, (state[0] if last else state)


def picked(slab, t):
    def kernel(slab, jumps, wraps, out, arrived):
        mine = pl.ds(slab[0] * SEND_TILES, SEND_TILES)
        copies = [
            pltpu.make_async_copy(table.at[mine], out.at[i], arrived.at[i])
            for i, table in enumerate((jumps, wraps))
        ]
        for copy in copies:
            copy.start()
        for copy in copies:
            copy.wait()

    tables = [pltpu.with_memory_space_constraint(t[name], pltpu.HBM) for name in ("jump", "wrap")]
    return call(
        kernel,
        "pick",
        [slab, *tables],
        pltpu.VMEM((2, SEND_TILES, 8, 128), F32),
        [SMEM, HBM, HBM],
        scratch_shapes=[pltpu.SemaphoreType.DMA((2,))],
    )


def solved(slab, moments, tables, t):
    def kernel(slab, moments, tables, zero, out, mean):
        me = slab[0]
        for slot in range(SEND_TILES):
            leftward = me * SEND_TILES + slot >= 2 * MODE_TILES
            place = lambda p: jnp.where(leftward, SLABS - 1 - p, p)
            values = [moments[place(p), slot] for p in range(SLABS)]
            r = tables[0, slot]
            run = values[0]
            for p in range(1, SLABS):
                run = run * r + values[p]
            run = run * tables[1, slot]
            for p in range(SLABS):
                out[place(p), slot] = run
                run = values[p] + r * run
        for pair in range(2):
            total = jnp.zeros((24, 128), F32)
            for p in range(SLABS):
                apart = lax.rem(me - p + SLABS, SLABS)
                total = total + zero[apart] * moments[p, SEND_TILES, pair : pair + 1, :]
            mean[pair] = jnp.broadcast_to(jnp.sum(total, axis=1, keepdims=True), (24, 128))

    return call(
        kernel,
        "solve",
        [slab, moments, *kept_close([tables, t["zero"]])],
        [f32_shape(SLABS, SEND_TILES, 8, 128), f32_shape(2, 24, 128)],
        [SMEM, VMEM, VMEM, VMEM],
    )


def products(g, core, own, swap, vis, field, before, coming, mean, state, t):
    first, whole = state is None, before is not None

    def kernel(core, own, swap, vis, fields, mean, edge, ratio, scale, table, hartley, *refs):
        if whole:
            before = refs[0]
            refs = refs[1:]
        if first:
            tiles = [[refs[0][divmod(MODE_TILES * n + i, SEND_TILES)] for i in range(MODE_TILES)] for n in range(4)]
            edges = [from_tiles(list_) for list_ in tiles]
            refs = refs[1:]
        else:
            edges = [refs[n // 2][n % 2] for n in range(4)]
            refs = refs[2:]
        sent, crossed, kept, right, left = refs
        rights, lefts = edges[:2], edges[2:]
        second = core[0] == 1
        h, r, c, x_table, owner = hartley[...], ratio[...], scale[...], table[...], strip()
        row = lax.broadcasted_iota(jnp.int32, (NG, WIDE), 0)
        lane = lax.broadcasted_iota(jnp.int32, (NG, WIDE), 1)
        corner = (row == 0) & (lane == 0)
        count = GROUPS[g] * PLANES
        sums = [[], []]
        for pair in range(2):
            run = before[pair] if whole else None
            for z in range(count):
                run = fields[pair, z] if run is None else r * run + fields[pair, z]
                sums[pair].append(run)
        for k in reversed(range(GROUPS[g])):
            start = k * (PLANES + 1)
            rests = [None, None]

            def share(p, x, y):
                resident, partner, visiting = own[p], swap[p], vis[p]
                extra = y * partner
                sent[p] = x * resident + jnp.where(second, extra, 0.0)
                kept[p] = x * visiting + jnp.where(second, 0.0, extra)
                crossed[p] = y * jnp.where(second, visiting, resident)

            for j in reversed(range(PLANES)):
                z = PLANES * k + j
                along_y = []
                for pair in range(2):
                    run = r * lefts[pair]
                    value = c * (sums[pair][z] + run) + edge[z] * rights[pair]
                    lefts[pair] = run + fields[pair, z]
                    middle = mean[pair, PLANES * FIRST[g] + z : PLANES * FIRST[g] + z + 1, :1]
                    value = jnp.where(corner, jnp.broadcast_to(middle, (NG, WIDE)), value)
                    along_y.append(table_times(h, value))
                both = times_table(jnp.concatenate(along_y, axis=0), x_table)
                parts = [both[:NG], both[NG:]]
                for pair in range(2):
                    rest = parts[pair][:, 128:]
                    rests[pair] = rest if rests[pair] is None else jnp.where(owner == j, rest, rests[pair])
                share(start + j, parts[0][:, :128], parts[1][:, :128])
            share(start + PLANES, *rests)
        for pair in range(2):
            right[pair] = rights[pair]
            left[pair] = lefts[pair]

    count = GROUPS[g] * PLANES
    edge = t["edge"][PLANES * FIRST[g] : PLANES * FIRST[g] + count]
    operands = [core, *at(g, [own]), *at(g, [swap, vis]), *kept_close([field]), mean]
    operands += kept_close([edge, t["ratio"], t["scale"], t["inverse"], t["hartley"]])
    if whole:
        operands += kept_close([before])
    operands += [coming] if first else kept_close(state)
    planes = space(g)((2, NG, WIDE), F32)
    sent, crossed, kept, *state = call(
        kernel,
        f"products_{g}",
        operands,
        [group_shape(g)] * 3 + [planes] * 2,
        [SMEM] + [VMEM] * (len(operands) - 1),
    )
    return sent, crossed, kept, state


def finished(g, kept, crossed, returned, result):
    def kernel(kept, crossed, returned, *refs):
        out = refs[-1]
        total = kept[...] + crossed[...] + returned[...]
        out[0, :, :, :128] = total[:PLANES]
        rest = total[PLANES]
        for j in range(PLANES):
            moved = rest if j == 0 else pltpu.roll(rest, 128 - 32 * j, 1)
            out[0, j, :, 128:] = moved[:, :32]

    block = pl.BlockSpec((PLANES + 1, NG, 128), lambda i: (i, 0, 0))
    operands = [kept, crossed, returned]
    specs = [block] * 3
    aliases = {}
    if result is not None:
        operands.append(result)
        specs.append(HBM)
        aliases = {3: 0}
    return call(
        kernel,
        f"finish_{g}",
        operands,
        pltpu.HBM((1, DEPTH, NG, NG), F32),
        specs,
        pl.BlockSpec((1, PLANES, NG, NG), lambda i: (0, FIRST[g] + i, 0, 0)),
        grid=(GROUPS[g],),
        input_output_aliases=aliases,
    )


def exchanged(array):
    flat = array.reshape(-1, 128)
    return lax.all_to_all(flat, "slab", 0, 0, tiled=True).reshape(array.shape)


def moved(name, array, pairs):
    with jax.named_scope(name):
        return lax.ppermute(array, "band", pairs)


def shards(orbitals):
    t = {name: jnp.asarray(table) for name, table in tables().items()}
    bands = lax.axis_size("band")
    core = lax.rem(lax.axis_index("band"), 2).astype(jnp.int32).reshape(1)
    slab = lax.axis_index("slab").astype(jnp.int32).reshape(1)
    outward = [(g, (g - 2) % bands if g % 2 == 0 else (g + 2) % bands) for g in range(bands)]
    homeward = [(b, a) for a, b in outward]
    across = [(g, g ^ 1) for g in range(bands)]

    groups = range(len(GROUPS))
    own = [packed(orbitals, g) for g in groups]
    vis = [moved(f"visit_{g}", own[g], outward) for g in groups]
    swap = [moved(f"swap_{g}", own[g], across) for g in groups]

    fields, befores, state = [], [], None
    for g in groups:
        befores.append(state and state[0])
        field, state = transformed(g, core, own[g], swap[g], vis[g], state, t)
        fields.append(field)
    state, slab, core, mine = lax.optimization_barrier((state, slab, core, picked(slab, t)))
    coming, mean = solved(slab, exchanged(state), mine, t)
    coming = exchanged(coming)

    def at_group(g, state):
        return products(g, core, own[g], swap[g], vis[g], fields[g], befores[g], coming, mean, state, t)

    def home(g, part):
        return moved(f"return_{g}", part, homeward)

    def cross(g, part):
        return moved(f"cross_{g}", part, across)

    sent, partner_2, kept_2, state = at_group(2, None)
    returned_2 = home(2, sent)
    sent, partner, kept_1, state = at_group(1, state)
    partner_2, partner = lax.optimization_barrier((partner_2, partner))
    returned_1 = home(1, sent)
    crossed_2, crossed_1 = cross(2, partner_2), cross(1, partner)
    returned_2, *state = lax.optimization_barrier((returned_2, *state))
    sent, partner, kept_0, state = at_group(0, state)
    returned_0, crossed_0 = home(0, sent), cross(0, partner)
    result = finished(2, kept_2, crossed_2, returned_2, None)
    result = finished(1, kept_1, crossed_1, returned_1, result)
    return finished(0, kept_0, crossed_0, returned_0, result)


def solution(mesh):
    spec = P("band", "slab", None, None)
    return jax.shard_map(shards, mesh=mesh, in_specs=(spec,), out_specs=spec, check_vma=False)
```

```python
import functools

import jax
import jax.numpy as jnp
import ml_dtypes
import numpy as np
from jax import lax
from jax.experimental import pallas as pl
from jax.experimental.pallas import tpu as pltpu
from jax.sharding import PartitionSpec as P

NG = 160
SLABS = 8
DEPTH = NG // SLABS
PLANES = 4
CHUNKS = DEPTH // PLANES
WIDE = 256
MODE_TILES = NG * NG // 1024
SEND_TILES = 13
F32 = jnp.float32
BF16 = jnp.bfloat16


def split_table(table):
    high = table.astype(np.float32).astype(ml_dtypes.bfloat16)
    low = (table - high.astype(np.float64)).astype(np.float32).astype(ml_dtypes.bfloat16)
    return high, low


def stacked(table, axis):
    high, low = split_table(table)
    return np.concatenate([high, high, low] if axis == 0 else [high, low, high], axis=axis)


def plane_tiles(plane):
    main = plane[:, :128].reshape(-1, 8, 128)
    rest = np.concatenate([plane[40 * g : 40 * g + 40, 128:] for g in range(4)], axis=1)
    return np.concatenate([main, rest.reshape(-1, 8, 128)])


def widened(plane):
    return np.pad(plane, [(0, 0)] * (plane.ndim - 1) + [(0, WIDE - NG)])


@functools.cache
def tables():
    index = np.arange(NG)
    angle = 2.0 * np.pi * (index[:, None] * index[None, :] % NG) / NG
    hartley = np.cos(angle) + np.sin(angle)
    forward = np.zeros((WIDE, WIDE))
    forward[:128, :NG] = hartley[:128]
    forward[128:, :NG] = np.tile(hartley[128:], (PLANES, 1))
    inverse = np.zeros((WIDE, WIDE))
    inverse[:NG, :128] = hartley[:, :128]
    inverse[:NG, 128:] = np.tile(hartley[:, 128:], (1, PLANES))
    wave = 4.0 * np.sin(np.pi * index / NG) ** 2
    lam = wave[:, None] + wave[None, :]
    ratio = 1.0 / (1.0 + lam / 2 + np.sqrt(lam + lam * lam / 4))
    ratio[0, 0] = 0.0
    scale = ratio / (1.0 - ratio**2) / NG**2
    powers = np.stack([ratio ** (PLANES * k) for k in range(CHUNKS)])
    edge = np.stack([scale * ratio ** (i + 1) for i in range(DEPTH)])
    jump = np.tile(plane_tiles(ratio**DEPTH), (4, 1, 1))
    wrap = np.tile(plane_tiles(1.0 / (1.0 - ratio**NG)), (4, 1, 1))
    spare = [(0, SLABS * SEND_TILES - 4 * MODE_TILES), (0, 0), (0, 0)]
    zero = np.zeros((SLABS, 24, 128))
    for apart in range(SLABS):
        for i in range(DEPTH):
            d = (DEPTH * apart + i - np.arange(DEPTH)) % NG
            zero[apart, i, :DEPTH] = ((NG**2 - 1) / (12 * NG) - d * (NG - d) / (2 * NG)) / NG**2
    as32 = lambda a: a.astype(np.float32)
    return dict(
        forward=stacked(forward, 0),
        inverse=stacked(inverse, 0),
        hartley=stacked(hartley, 1),
        ratio=as32(widened(ratio)),
        scale=as32(widened(scale)),
        powers=as32(widened(powers)),
        edge=as32(widened(edge)),
        jump=as32(np.pad(jump, spare)),
        wrap=as32(np.pad(wrap, spare)),
        zero=as32(zero),
    )


def split(value):
    high = value.astype(BF16)
    return high, (value - high.astype(F32)).astype(BF16)


def dot(a, b):
    return jnp.dot(a, b, preferred_element_type=F32)


def times_table(value, table):
    high, low = split(value)
    return dot(jnp.concatenate([high, low, high], axis=1), table)


def table_times(table, value):
    high, low = split(value)
    return dot(table, jnp.concatenate([high, high, low], axis=0))


VMEM = pl.BlockSpec(memory_space=pltpu.VMEM)
SMEM = pl.BlockSpec(memory_space=pltpu.SMEM)
HBM = pl.BlockSpec(memory_space=pltpu.HBM)
GROUPS = (2, 2, 1)
FIRST = tuple(sum(GROUPS[:g]) for g in range(len(GROUPS)))


def call(kernel, name, operands, outs, in_specs=None, out_specs=VMEM, limit=14, **kwargs):
    if in_specs is None:
        in_specs = [VMEM] * len(operands)
    return pl.pallas_call(
        kernel,
        name=name,
        out_shape=outs,
        in_specs=in_specs,
        out_specs=jax.tree.map(lambda a: out_specs, outs),
        compiler_params=pltpu.CompilerParams(vmem_limit_bytes=limit * 2**20),
        cost_estimate=pl.CostEstimate(flops=1, bytes_accessed=1, transcendentals=0),
        **kwargs,
    )(*operands)


def at(g, arrays):
    place = pltpu.VMEM if g == len(GROUPS) - 1 else pltpu.HBM
    return [pltpu.with_memory_space_constraint(a, place) for a in arrays]


def kept_close(arrays):
    return [pltpu.with_memory_space_constraint(a, pltpu.VMEM) for a in arrays]


def space(g):
    return pltpu.VMEM


def resting(g):
    return pltpu.HBM if g == 0 else pltpu.VMEM


def f32_shape(*shape):
    return jax.ShapeDtypeStruct(shape, F32)


def group_shape(g):
    return space(g)((GROUPS[g] * (PLANES + 1), NG, 128), F32)


def own_shape(g):
    return pltpu.HBM((GROUPS[g] * (PLANES + 1), NG, 128), F32) if g == 1 else group_shape(g)


def packed(orbitals, g):
    count = GROUPS[g]
    close = g != 1

    def kernel(orbitals, out, block, *refs):
        ready, (arrived, gone) = (out, refs) if close else (refs[0], refs[1:])
        comes, goes = [], []
        for c in range(count):
            there = pl.ds((FIRST[g] + c) * PLANES, PLANES)
            here = pl.ds(c * PLANES, PLANES)
            comes.append(pltpu.make_async_copy(orbitals.at[0, there], block.at[here], arrived.at[c]))
            comes[c].start()
        for c in range(count):
            comes[c].wait()
            base = c * (PLANES + 1)
            planes = range(c * PLANES, (c + 1) * PLANES)
            for j, z in enumerate(planes):
                ready[base + j] = block[z, :, :128]
            ready[base + PLANES] = jnp.concatenate([block[z, :, 128:] for z in planes], axis=1)
            if not close:
                part = pl.ds(base, PLANES + 1)
                goes.append(pltpu.make_async_copy(ready.at[part], out.at[part], gone.at[c]))
                goes[c].start()
        for copy in goes:
            copy.wait()

    scratch = [pltpu.VMEM((count * PLANES, NG, NG), F32)]
    if not close:
        scratch.append(pltpu.VMEM(group_shape(g).shape, F32))
    return call(
        kernel,
        f"pack_{g}",
        [pltpu.with_memory_space_constraint(orbitals, pltpu.HBM)],
        own_shape(g),
        [HBM],
        VMEM if close else HBM,
        scratch_shapes=scratch + [pltpu.SemaphoreType.DMA((count,))] * 2,
    )


def fetched(array):
    def kernel(array, out, arrived):
        copy = pltpu.make_async_copy(array, out, arrived)
        copy.start()
        copy.wait()

    return call(
        kernel,
        "fetch",
        [pltpu.with_memory_space_constraint(array, pltpu.HBM)],
        pltpu.VMEM(array.shape, F32),
        [HBM],
        scratch_shapes=[pltpu.SemaphoreType.DMA],
    )


def strip():
    return lax.broadcasted_iota(jnp.int32, (NG, 128), 1) // (128 // PLANES)


def to_tiles(plane):
    rest = plane[:, 128:]
    moved = rest[:40]
    for g in range(1, 4):
        moved = moved + pltpu.roll(rest[40 * g : 40 * g + 40], 32 * g, 1)
    return plane[:, :128].reshape(-1, 8, 128), moved.reshape(-1, 8, 128)


def from_tiles(tiles):
    main = jnp.concatenate(tiles[:20], axis=0)
    rest = jnp.concatenate(tiles[20:], axis=0)
    lane = lax.broadcasted_iota(jnp.int32, rest.shape, 1)
    parts = [rest] + [pltpu.roll(rest, 128 - 32 * g, 1) for g in range(1, 4)]
    rest = jnp.concatenate([jnp.where(lane < 32, part, 0.0) for part in parts], axis=0)
    return jnp.concatenate([main, rest], axis=1)


def transformed(g, core, own, swap, vis, state, t):
    first, last = g == 0, g == len(GROUPS) - 1

    def kernel(*refs):
        core, own, swap, vis, table, hartley, ratio, powers = refs[:8]
        refs = refs[8:]
        if not first:
            right0, left0, zero0 = refs[:3]
            refs = refs[3:]
        fields, *results = refs
        second = core[0] == 1
        h, r, x_table, owner = hartley[...], ratio[...], table[...], strip()
        row = lax.broadcasted_iota(jnp.int32, (8, 128), 0)
        lane = lax.broadcasted_iota(jnp.int32, (8, 128), 1)
        means = jnp.zeros((8, 128), F32) if first else zero0[...]
        rights = [None if first else right0[pair] for pair in range(2)]
        lefts = [None if first else left0[pair] for pair in range(2)]
        for c in range(GROUPS[g]):
            start = c * (PLANES + 1)
            densities = []
            for p in range(start, start + PLANES + 1):
                other = jnp.where(second, vis[p], own[p])
                densities.append((own[p] * vis[p], other * swap[p]))
            for j in range(PLANES):
                wide = [
                    jnp.concatenate([densities[j][pair], jnp.where(owner == j, densities[PLANES][pair], 0.0)], axis=1)
                    for pair in range(2)
                ]
                along_x = times_table(jnp.concatenate(wide, axis=0), x_table)
                z = PLANES * c + j
                for pair in range(2):
                    field = table_times(h, along_x[NG * pair : NG * (pair + 1)])
                    fields[pair, z] = field
                    rights[pair] = field if rights[pair] is None else r * rights[pair] + field
                    here = (row == pair) & (lane == PLANES * FIRST[g] + z)
                    means = jnp.where(here, jnp.broadcast_to(field[:1, :1], (8, 128)), means)
            for pair in range(2):
                back = fields[pair, PLANES * c + PLANES - 1]
                for j in reversed(range(PLANES - 1)):
                    back = r * back + fields[pair, PLANES * c + j]
                lefts[pair] = back if lefts[pair] is None else lefts[pair] + powers[FIRST[g] + c] * back
        if not last:
            right, left, zero = results
            for pair in range(2):
                right[pair] = rights[pair]
                left[pair] = lefts[pair]
            zero[...] = means
            return
        (out,) = results
        for number, plane in enumerate(rights + lefts):
            main, rest = to_tiles(plane)
            for i in range(MODE_TILES):
                tile = main[i] if i < 20 else rest[i - 20]
                to, slot = divmod(MODE_TILES * number + i, SEND_TILES)
                out[to, slot] = tile
        for i in range(4 * MODE_TILES, SLABS * SEND_TILES):
            out[i // SEND_TILES, i % SEND_TILES] = jnp.zeros((8, 128), F32)
        for to in range(SLABS):
            out[to, SEND_TILES] = means

    outs = [resting(g)((2, GROUPS[g] * PLANES, NG, WIDE), F32)]
    if last:
        outs += [f32_shape(SLABS, SEND_TILES + 1, 8, 128)]
    else:
        outs += [space(g + 1)((2, NG, WIDE), F32)] * 2 + [f32_shape(8, 128)]
    operands = [core, *(at(g, [own]) if g == 1 else kept_close([own])), *at(g, [swap, vis])]
    operands += kept_close([t["forward"], t["hartley"], t["ratio"], t["powers"]])
    if not first:
        operands += [*kept_close(state[:2]), state[2]]
    field, *state = call(
        kernel, f"forward_{g}", operands, outs, [SMEM] + [VMEM] * (len(operands) - 1)
    )
    return field, (state[0] if last else state)


def picked(slab, t):
    def kernel(slab, jumps, wraps, out, arrived):
        mine = pl.ds(slab[0] * SEND_TILES, SEND_TILES)
        copies = [
            pltpu.make_async_copy(table.at[mine], out.at[i], arrived.at[i])
            for i, table in enumerate((jumps, wraps))
        ]
        for copy in copies:
            copy.start()
        for copy in copies:
            copy.wait()

    tables = [pltpu.with_memory_space_constraint(t[name], pltpu.HBM) for name in ("jump", "wrap")]
    return call(
        kernel,
        "pick",
        [slab, *tables],
        pltpu.VMEM((2, SEND_TILES, 8, 128), F32),
        [SMEM, HBM, HBM],
        scratch_shapes=[pltpu.SemaphoreType.DMA((2,))],
    )


def solved(slab, moments, tables, t):
    def kernel(slab, moments, tables, zero, out, mean):
        me = slab[0]
        for slot in range(SEND_TILES):
            leftward = me * SEND_TILES + slot >= 2 * MODE_TILES
            place = lambda p: jnp.where(leftward, SLABS - 1 - p, p)
            values = [moments[place(p), slot] for p in range(SLABS)]
            r = tables[0, slot]
            run = values[0]
            for p in range(1, SLABS):
                run = run * r + values[p]
            run = run * tables[1, slot]
            for p in range(SLABS):
                out[place(p), slot] = run
                run = values[p] + r * run
        for pair in range(2):
            total = jnp.zeros((24, 128), F32)
            for p in range(SLABS):
                apart = lax.rem(me - p + SLABS, SLABS)
                total = total + zero[apart] * moments[p, SEND_TILES, pair : pair + 1, :]
            mean[pair] = jnp.broadcast_to(jnp.sum(total, axis=1, keepdims=True), (24, 128))

    return call(
        kernel,
        "solve",
        [slab, moments, *kept_close([tables, t["zero"]])],
        [f32_shape(SLABS, SEND_TILES, 8, 128), f32_shape(2, 24, 128)],
        [SMEM, VMEM, VMEM, VMEM],
    )


def products(g, core, own, swap, vis, field, before, coming, mean, state, t):
    first, whole = state is None, before is not None

    def kernel(core, own, swap, vis, fields, mean, edge, ratio, scale, table, hartley, *refs):
        if whole:
            before = refs[0]
            refs = refs[1:]
        if first:
            tiles = [[refs[0][divmod(MODE_TILES * n + i, SEND_TILES)] for i in range(MODE_TILES)] for n in range(4)]
            edges = [from_tiles(list_) for list_ in tiles]
            refs = refs[1:]
        else:
            edges = [refs[n // 2][n % 2] for n in range(4)]
            refs = refs[2:]
        sent, crossed, kept, right, left = refs
        rights, lefts = edges[:2], edges[2:]
        second = core[0] == 1
        h, r, c, x_table, owner = hartley[...], ratio[...], scale[...], table[...], strip()
        count = GROUPS[g] * PLANES
        sums = [[], []]
        for pair in range(2):
            run = before[pair] if whole else None
            for z in range(count):
                run = fields[pair, z] if run is None else r * run + fields[pair, z]
                sums[pair].append(run)
        for k in reversed(range(GROUPS[g])):
            start = k * (PLANES + 1)
            rests = [None, None]

            def share(p, x, y):
                resident, partner, visiting = own[p], swap[p], vis[p]
                extra = y * partner
                sent[p] = x * resident + jnp.where(second, extra, 0.0)
                kept[p] = x * visiting + jnp.where(second, 0.0, extra)
                crossed[p] = y * jnp.where(second, visiting, resident)

            for j in reversed(range(PLANES)):
                z = PLANES * k + j
                along_y = []
                for pair in range(2):
                    run = r * lefts[pair]
                    value = c * (sums[pair][z] + run) + edge[z] * rights[pair]
                    lefts[pair] = run + fields[pair, z]
                    along_y.append(table_times(h, value))
                both = times_table(jnp.concatenate(along_y, axis=0), x_table)
                middles = [mean[pair, PLANES * FIRST[g] + z : PLANES * FIRST[g] + z + 1, :1] for pair in range(2)]
                parts = [both[:NG] + middles[0], both[NG:] + middles[1]]
                for pair in range(2):
                    rest = parts[pair][:, 128:]
                    rests[pair] = rest if rests[pair] is None else jnp.where(owner == j, rest, rests[pair])
                share(start + j, parts[0][:, :128], parts[1][:, :128])
            share(start + PLANES, *rests)
        for pair in range(2):
            right[pair] = rights[pair]
            left[pair] = lefts[pair]

    count = GROUPS[g] * PLANES
    edge = t["edge"][PLANES * FIRST[g] : PLANES * FIRST[g] + count]
    operands = [core, *(at(g, [own]) if g == 1 else kept_close([own])), *at(g, [swap, vis]), *([pltpu.with_memory_space_constraint(field, pltpu.HBM)] if g == 0 else kept_close([field])), mean]
    operands += kept_close([edge, t["ratio"], t["scale"], t["inverse"], t["hartley"]])
    if whole:
        operands += kept_close([before])
    operands += [coming] if first else kept_close(state)
    planes = space(g)((2, NG, WIDE), F32)
    sent, crossed, kept, *state = call(
        kernel,
        f"products_{g}",
        operands,
        [group_shape(g)] * 3 + [planes] * 2,
        [SMEM] + [VMEM] * (len(operands) - 1),
    )
    return sent, crossed, kept, state


def finished(g, kept, crossed, returned, result):
    def kernel(kept, crossed, returned, *refs):
        out = refs[-1]
        total = kept[...] + crossed[...] + returned[...]
        out[0, :, :, :128] = total[:PLANES]
        rest = total[PLANES]
        for j in range(PLANES):
            moved = rest if j == 0 else pltpu.roll(rest, 128 - 32 * j, 1)
            out[0, j, :, 128:] = moved[:, :32]

    block = pl.BlockSpec((PLANES + 1, NG, 128), lambda i: (i, 0, 0))
    operands = [kept, crossed, returned]
    specs = [block] * 3
    aliases = {}
    if result is not None:
        operands.append(result)
        specs.append(HBM)
        aliases = {3: 0}
    return call(
        kernel,
        f"finish_{g}",
        operands,
        pltpu.HBM((1, DEPTH, NG, NG), F32),
        specs,
        pl.BlockSpec((1, PLANES, NG, NG), lambda i: (0, FIRST[g] + i, 0, 0)),
        grid=(GROUPS[g],),
        input_output_aliases=aliases,
    )


def exchanged(array):
    flat = array.reshape(-1, 128)
    return lax.all_to_all(flat, "slab", 0, 0, tiled=True).reshape(array.shape)


def moved(name, array, pairs):
    with jax.named_scope(name):
        return lax.ppermute(array, "band", pairs)


def shards(orbitals):
    t = {name: jnp.asarray(table) for name, table in tables().items()}
    bands = lax.axis_size("band")
    core = lax.rem(lax.axis_index("band"), 2).astype(jnp.int32).reshape(1)
    slab = lax.axis_index("slab").astype(jnp.int32).reshape(1)
    outward = [(g, (g - 2) % bands if g % 2 == 0 else (g + 2) % bands) for g in range(bands)]
    homeward = [(b, a) for a, b in outward]
    across = [(g, g ^ 1) for g in range(bands)]

    groups = range(len(GROUPS))
    own = [packed(orbitals, g) for g in groups]
    vis = [moved(f"visit_{g}", own[g], outward) for g in groups]
    swap = [moved(f"swap_{g}", own[g], across) for g in groups]

    fields, befores, state = [], [], None
    for g in groups:
        if g == 1:
            swap[2], *state = lax.optimization_barrier((fetched(swap[2]), *state))
        befores.append(state and state[0])
        field, state = transformed(g, core, own[g], swap[g], vis[g], state, t)
        fields.append(field)
    state, slab, core, mine = lax.optimization_barrier((state, slab, core, picked(slab, t)))
    coming, mean = solved(slab, exchanged(state), mine, t)
    coming = exchanged(coming)

    def at_group(g, state):
        return products(g, core, own[g], swap[g], vis[g], fields[g], befores[g], coming, mean, state, t)

    def home(g, part):
        return moved(f"return_{g}", part, homeward)

    def cross(g, part):
        return moved(f"cross_{g}", part, across)

    sent, partner_2, kept_2, state = at_group(2, None)
    returned_2 = home(2, sent)
    sent, partner, kept_1, state = at_group(1, state)
    partner_2, partner = lax.optimization_barrier((partner_2, partner))
    returned_1 = home(1, sent)
    crossed_2, crossed_1 = cross(2, partner_2), cross(1, partner)
    returned_2, *state = lax.optimization_barrier((returned_2, *state))
    sent, partner, kept_0, state = at_group(0, state)
    returned_0, crossed_0 = home(0, sent), cross(0, partner)
    result = finished(2, kept_2, crossed_2, returned_2, None)
    result = finished(1, kept_1, crossed_1, returned_1, result)
    return finished(0, kept_0, crossed_0, returned_0, result)


def solution(mesh):
    spec = P("band", "slab", None, None)
    return jax.shard_map(shards, mesh=mesh, in_specs=(spec,), out_specs=spec, check_vma=False)
```

```python
import functools

import jax
import jax.numpy as jnp
import ml_dtypes
import numpy as np
from jax import lax
from jax.experimental import pallas as pl
from jax.experimental.pallas import tpu as pltpu
from jax.sharding import PartitionSpec as P

NG = 160
SLABS = 8
DEPTH = NG // SLABS
PLANES = 4
CHUNKS = DEPTH // PLANES
WIDE = 256
MODE_TILES = NG * NG // 1024
SEND_TILES = 13
F32 = jnp.float32
BF16 = jnp.bfloat16


def split_table(table):
    high = table.astype(np.float32).astype(ml_dtypes.bfloat16)
    low = (table - high.astype(np.float64)).astype(np.float32).astype(ml_dtypes.bfloat16)
    return high, low


def stacked(table, axis):
    high, low = split_table(table)
    return np.concatenate([high, high, low] if axis == 0 else [high, low, high], axis=axis)


def plane_tiles(plane):
    main = plane[:, :128].reshape(-1, 8, 128)
    rest = np.concatenate([plane[40 * g : 40 * g + 40, 128:] for g in range(4)], axis=1)
    return np.concatenate([main, rest.reshape(-1, 8, 128)])


def widened(plane):
    return np.pad(plane, [(0, 0)] * (plane.ndim - 1) + [(0, WIDE - NG)])


@functools.cache
def tables():
    index = np.arange(NG)
    angle = 2.0 * np.pi * (index[:, None] * index[None, :] % NG) / NG
    hartley = np.cos(angle) + np.sin(angle)
    forward = np.zeros((WIDE, WIDE))
    forward[:128, :NG] = hartley[:128]
    forward[128:, :NG] = np.tile(hartley[128:], (PLANES, 1))
    inverse = np.zeros((WIDE, WIDE))
    inverse[:NG, :128] = hartley[:, :128]
    inverse[:NG, 128:] = np.tile(hartley[:, 128:], (1, PLANES))
    wave = 4.0 * np.sin(np.pi * index / NG) ** 2
    lam = wave[:, None] + wave[None, :]
    ratio = 1.0 / (1.0 + lam / 2 + np.sqrt(lam + lam * lam / 4))
    ratio[0, 0] = 0.0
    scale = ratio / (1.0 - ratio**2) / NG**2
    powers = np.stack([ratio ** (PLANES * k) for k in range(CHUNKS)])
    edge = np.stack([scale * ratio ** (i + 1) for i in range(DEPTH)])
    jump = np.tile(plane_tiles(ratio**DEPTH), (4, 1, 1))
    wrap = np.tile(plane_tiles(1.0 / (1.0 - ratio**NG)), (4, 1, 1))
    spare = [(0, SLABS * SEND_TILES - 4 * MODE_TILES), (0, 0), (0, 0)]
    zero = np.zeros((SLABS, 24, 128))
    for apart in range(SLABS):
        for i in range(DEPTH):
            d = (DEPTH * apart + i - np.arange(DEPTH)) % NG
            zero[apart, i, :DEPTH] = ((NG**2 - 1) / (12 * NG) - d * (NG - d) / (2 * NG)) / NG**2
    as32 = lambda a: a.astype(np.float32)
    return dict(
        forward=stacked(forward, 0),
        inverse=stacked(inverse, 0),
        hartley=stacked(hartley, 1),
        ratio=as32(widened(ratio)),
        scale=as32(widened(scale)),
        powers=as32(widened(powers)),
        edge=as32(widened(edge)),
        jump=as32(np.pad(jump, spare)),
        wrap=as32(np.pad(wrap, spare)),
        zero=as32(zero),
    )


def split(value):
    high = value.astype(BF16)
    return high, (value - high.astype(F32)).astype(BF16)


def dot(a, b):
    return jnp.dot(a, b, preferred_element_type=F32)


def times_table(value, table):
    high, low = split(value)
    return dot(jnp.concatenate([high, low, high], axis=1), table)


def table_times(table, value):
    high, low = split(value)
    return dot(table, jnp.concatenate([high, high, low], axis=0))


VMEM = pl.BlockSpec(memory_space=pltpu.VMEM)
SMEM = pl.BlockSpec(memory_space=pltpu.SMEM)
HBM = pl.BlockSpec(memory_space=pltpu.HBM)
GROUPS = (2, 2, 1)
FIRST = tuple(sum(GROUPS[:g]) for g in range(len(GROUPS)))


def call(kernel, name, operands, outs, in_specs=None, out_specs=VMEM, limit=14, **kwargs):
    if in_specs is None:
        in_specs = [VMEM] * len(operands)
    return pl.pallas_call(
        kernel,
        name=name,
        out_shape=outs,
        in_specs=in_specs,
        out_specs=jax.tree.map(lambda a: out_specs, outs),
        compiler_params=pltpu.CompilerParams(vmem_limit_bytes=limit * 2**20),
        cost_estimate=pl.CostEstimate(flops=1, bytes_accessed=1, transcendentals=0),
        **kwargs,
    )(*operands)


def at(g, arrays):
    place = pltpu.VMEM if g == len(GROUPS) - 1 else pltpu.HBM
    return [pltpu.with_memory_space_constraint(a, place) for a in arrays]


def kept_close(arrays):
    return [pltpu.with_memory_space_constraint(a, pltpu.VMEM) for a in arrays]


def space(g):
    return pltpu.VMEM


def resting(g):
    return pltpu.VMEM


def f32_shape(*shape):
    return jax.ShapeDtypeStruct(shape, F32)


def group_shape(g):
    return space(g)((GROUPS[g] * (PLANES + 1), NG, 128), F32)


def own_shape(g):
    return pltpu.HBM((GROUPS[g] * (PLANES + 1), NG, 128), F32) if g == 1 else group_shape(g)


def packed(orbitals, g):
    count = GROUPS[g]
    close = g != 1

    def kernel(orbitals, out, block, *refs):
        ready, (arrived, gone) = (out, refs) if close else (refs[0], refs[1:])
        comes, goes = [], []
        for c in range(count):
            there = pl.ds((FIRST[g] + c) * PLANES, PLANES)
            here = pl.ds(c * PLANES, PLANES)
            comes.append(pltpu.make_async_copy(orbitals.at[0, there], block.at[here], arrived.at[c]))
            comes[c].start()
        for c in range(count):
            comes[c].wait()
            base = c * (PLANES + 1)
            planes = range(c * PLANES, (c + 1) * PLANES)
            for j, z in enumerate(planes):
                ready[base + j] = block[z, :, :128]
            ready[base + PLANES] = jnp.concatenate([block[z, :, 128:] for z in planes], axis=1)
            if not close:
                part = pl.ds(base, PLANES + 1)
                goes.append(pltpu.make_async_copy(ready.at[part], out.at[part], gone.at[c]))
                goes[c].start()
        for copy in goes:
            copy.wait()

    scratch = [pltpu.VMEM((count * PLANES, NG, NG), F32)]
    if not close:
        scratch.append(pltpu.VMEM(group_shape(g).shape, F32))
    return call(
        kernel,
        f"pack_{g}",
        [pltpu.with_memory_space_constraint(orbitals, pltpu.HBM)],
        own_shape(g),
        [HBM],
        VMEM if close else HBM,
        scratch_shapes=scratch + [pltpu.SemaphoreType.DMA((count,))] * 2,
    )


def fetched(array):
    def kernel(array, out, arrived):
        copy = pltpu.make_async_copy(array, out, arrived)
        copy.start()
        copy.wait()

    return call(
        kernel,
        "fetch",
        [pltpu.with_memory_space_constraint(array, pltpu.HBM)],
        pltpu.VMEM(array.shape, F32),
        [HBM],
        scratch_shapes=[pltpu.SemaphoreType.DMA],
    )


def strip():
    return lax.broadcasted_iota(jnp.int32, (NG, 128), 1) // (128 // PLANES)


def to_tiles(plane):
    rest = plane[:, 128:]
    moved = rest[:40]
    for g in range(1, 4):
        moved = moved + pltpu.roll(rest[40 * g : 40 * g + 40], 32 * g, 1)
    return plane[:, :128].reshape(-1, 8, 128), moved.reshape(-1, 8, 128)


def from_tiles(tiles):
    main = jnp.concatenate(tiles[:20], axis=0)
    rest = jnp.concatenate(tiles[20:], axis=0)
    lane = lax.broadcasted_iota(jnp.int32, rest.shape, 1)
    parts = [rest] + [pltpu.roll(rest, 128 - 32 * g, 1) for g in range(1, 4)]
    rest = jnp.concatenate([jnp.where(lane < 32, part, 0.0) for part in parts], axis=0)
    return jnp.concatenate([main, rest], axis=1)


def transformed(g, core, own, swap, vis, state, t):
    first, last = g == 0, g == len(GROUPS) - 1

    def kernel(*refs):
        core, own, swap, vis, table, hartley, ratio, powers = refs[:8]
        refs = refs[8:]
        if not first:
            right0, left0, zero0 = refs[:3]
            refs = refs[3:]
        fields, *results = refs
        second = core[0] == 1
        h, r, x_table, owner = hartley[...], ratio[...], table[...], strip()
        row = lax.broadcasted_iota(jnp.int32, (8, 128), 0)
        lane = lax.broadcasted_iota(jnp.int32, (8, 128), 1)
        means = jnp.zeros((8, 128), F32) if first else zero0[...]
        rights = [None if first else right0[pair] for pair in range(2)]
        lefts = [None if first else left0[pair] for pair in range(2)]
        for c in range(GROUPS[g]):
            start = c * (PLANES + 1)
            densities = []
            for p in range(start, start + PLANES + 1):
                other = jnp.where(second, vis[p], own[p])
                densities.append((own[p] * vis[p], other * swap[p]))
            for j in range(PLANES):
                wide = [
                    jnp.concatenate([densities[j][pair], jnp.where(owner == j, densities[PLANES][pair], 0.0)], axis=1)
                    for pair in range(2)
                ]
                along_x = times_table(jnp.concatenate(wide, axis=0), x_table)
                z = PLANES * c + j
                for pair in range(2):
                    field = table_times(h, along_x[NG * pair : NG * (pair + 1)])
                    fields[pair, z] = field
                    rights[pair] = field if rights[pair] is None else r * rights[pair] + field
                    here = (row == pair) & (lane == PLANES * FIRST[g] + z)
                    means = jnp.where(here, jnp.broadcast_to(field[:1, :1], (8, 128)), means)
            for pair in range(2):
                back = fields[pair, PLANES * c + PLANES - 1]
                for j in reversed(range(PLANES - 1)):
                    back = r * back + fields[pair, PLANES * c + j]
                lefts[pair] = back if lefts[pair] is None else lefts[pair] + powers[FIRST[g] + c] * back
        if not last:
            right, left, zero = results
            for pair in range(2):
                right[pair] = rights[pair]
                left[pair] = lefts[pair]
            zero[...] = means
            return
        (out,) = results
        for number, plane in enumerate(rights + lefts):
            main, rest = to_tiles(plane)
            for i in range(MODE_TILES):
                tile = main[i] if i < 20 else rest[i - 20]
                to, slot = divmod(MODE_TILES * number + i, SEND_TILES)
                out[to, slot] = tile
        for i in range(4 * MODE_TILES, SLABS * SEND_TILES):
            out[i // SEND_TILES, i % SEND_TILES] = jnp.zeros((8, 128), F32)
        for to in range(SLABS):
            out[to, SEND_TILES] = means

    outs = [resting(g)((2, GROUPS[g] * PLANES, NG, WIDE), F32)]
    if last:
        outs += [f32_shape(SLABS, SEND_TILES + 1, 8, 128)]
    else:
        outs += [space(g + 1)((2, NG, WIDE), F32)] * 2 + [f32_shape(8, 128)]
    operands = [core, *(at(g, [own]) if g == 1 else kept_close([own])), *at(g, [swap, vis])]
    operands += kept_close([t["forward"], t["hartley"], t["ratio"], t["powers"]])
    if not first:
        operands += [*kept_close(state[:2]), state[2]]
    field, *state = call(
        kernel, f"forward_{g}", operands, outs, [SMEM] + [VMEM] * (len(operands) - 1)
    )
    return field, (state[0] if last else state)


def picked(slab, t):
    def kernel(slab, jumps, wraps, out, arrived):
        mine = pl.ds(slab[0] * SEND_TILES, SEND_TILES)
        copies = [
            pltpu.make_async_copy(table.at[mine], out.at[i], arrived.at[i])
            for i, table in enumerate((jumps, wraps))
        ]
        for copy in copies:
            copy.start()
        for copy in copies:
            copy.wait()

    tables = [pltpu.with_memory_space_constraint(t[name], pltpu.HBM) for name in ("jump", "wrap")]
    return call(
        kernel,
        "pick",
        [slab, *tables],
        pltpu.VMEM((2, SEND_TILES, 8, 128), F32),
        [SMEM, HBM, HBM],
        scratch_shapes=[pltpu.SemaphoreType.DMA((2,))],
    )


def solved(slab, moments, tables, t):
    def kernel(slab, moments, tables, zero, out, mean):
        me = slab[0]
        for slot in range(SEND_TILES):
            leftward = me * SEND_TILES + slot >= 2 * MODE_TILES
            place = lambda p: jnp.where(leftward, SLABS - 1 - p, p)
            values = [moments[place(p), slot] for p in range(SLABS)]
            r = tables[0, slot]
            run = values[0]
            for p in range(1, SLABS):
                run = run * r + values[p]
            run = run * tables[1, slot]
            for p in range(SLABS):
                out[place(p), slot] = run
                run = values[p] + r * run
        for pair in range(2):
            total = jnp.zeros((24, 128), F32)
            for p in range(SLABS):
                apart = lax.rem(me - p + SLABS, SLABS)
                total = total + zero[apart] * moments[p, SEND_TILES, pair : pair + 1, :]
            mean[pair] = jnp.broadcast_to(jnp.sum(total, axis=1, keepdims=True), (24, 128))

    return call(
        kernel,
        "solve",
        [slab, moments, *kept_close([tables, t["zero"]])],
        [f32_shape(SLABS, SEND_TILES, 8, 128), f32_shape(2, 24, 128)],
        [SMEM, VMEM, VMEM, VMEM],
    )


def products(g, core, own, swap, vis, field, before, coming, mean, state, t):
    first, whole = state is None, before is not None

    def kernel(core, own, swap, vis, fields, mean, edge, ratio, scale, table, hartley, *refs):
        if whole:
            before = refs[0]
            refs = refs[1:]
        if first:
            tiles = [[refs[0][divmod(MODE_TILES * n + i, SEND_TILES)] for i in range(MODE_TILES)] for n in range(4)]
            edges = [from_tiles(list_) for list_ in tiles]
            refs = refs[1:]
        else:
            edges = [refs[n // 2][n % 2] for n in range(4)]
            refs = refs[2:]
        sent, crossed, kept, right, left = refs
        rights, lefts = edges[:2], edges[2:]
        second = core[0] == 1
        h, r, c, x_table, owner = hartley[...], ratio[...], scale[...], table[...], strip()
        count = GROUPS[g] * PLANES
        sums = [[], []]
        for pair in range(2):
            run = before[pair] if whole else None
            for z in range(count):
                run = fields[pair, z] if run is None else r * run + fields[pair, z]
                sums[pair].append(run)
        for k in reversed(range(GROUPS[g])):
            start = k * (PLANES + 1)
            rests = [None, None]

            def share(p, x, y):
                resident, partner, visiting = own[p], swap[p], vis[p]
                extra = y * partner
                sent[p] = x * resident + jnp.where(second, extra, 0.0)
                kept[p] = x * visiting + jnp.where(second, 0.0, extra)
                crossed[p] = y * jnp.where(second, visiting, resident)

            for j in reversed(range(PLANES)):
                z = PLANES * k + j
                along_y = []
                for pair in range(2):
                    run = r * lefts[pair]
                    value = c * (sums[pair][z] + run) + edge[z] * rights[pair]
                    lefts[pair] = run + fields[pair, z]
                    along_y.append(table_times(h, value))
                both = times_table(jnp.concatenate(along_y, axis=0), x_table)
                middles = [mean[pair, PLANES * FIRST[g] + z : PLANES * FIRST[g] + z + 1, :1] for pair in range(2)]
                parts = [both[:NG] + middles[0], both[NG:] + middles[1]]
                for pair in range(2):
                    rest = parts[pair][:, 128:]
                    rests[pair] = rest if rests[pair] is None else jnp.where(owner == j, rest, rests[pair])
                share(start + j, parts[0][:, :128], parts[1][:, :128])
            share(start + PLANES, *rests)
        for pair in range(2):
            right[pair] = rights[pair]
            left[pair] = lefts[pair]

    count = GROUPS[g] * PLANES
    edge = t["edge"][PLANES * FIRST[g] : PLANES * FIRST[g] + count]
    operands = [core, *(at(g, [own]) if g == 1 else kept_close([own])), *at(g, [swap, vis]), *kept_close([field]), mean]
    operands += kept_close([edge, t["ratio"], t["scale"], t["inverse"], t["hartley"]])
    if whole:
        operands += kept_close([before])
    operands += [coming] if first else kept_close(state)
    planes = space(g)((2, NG, WIDE), F32)
    sent, crossed, kept, *state = call(
        kernel,
        f"products_{g}",
        operands,
        [group_shape(g)] * 3 + [planes] * 2,
        [SMEM] + [VMEM] * (len(operands) - 1),
    )
    return sent, crossed, kept, state


def finished(g, kept, crossed, returned, result):
    count = GROUPS[g]

    def kernel(kept, crossed, returned, *refs):
        out, block, gone = refs[-3:]
        copies = []
        for c in range(count):
            base = c * (PLANES + 1)
            rest = kept[base + PLANES] + crossed[base + PLANES] + returned[base + PLANES]
            for j in range(PLANES):
                z = c * PLANES + j
                block[z, :, :128] = kept[base + j] + crossed[base + j] + returned[base + j]
                moved = rest if j == 0 else pltpu.roll(rest, 128 - 32 * j, 1)
                block[z, :, 128:] = moved[:, :32]
            here = pl.ds(c * PLANES, PLANES)
            there = pl.ds((FIRST[g] + c) * PLANES, PLANES)
            copies.append(pltpu.make_async_copy(block.at[here], out.at[0, there], gone.at[c]))
            copies[c].start()
        for copy in copies:
            copy.wait()

    operands = [kept, crossed, returned]
    specs = [VMEM] * 3
    aliases = {}
    if result is not None:
        operands.append(result)
        specs.append(HBM)
        aliases = {3: 0}
    return call(
        kernel,
        f"finish_{g}",
        operands,
        pltpu.HBM((1, DEPTH, NG, NG), F32),
        specs,
        HBM,
        input_output_aliases=aliases,
        scratch_shapes=[pltpu.VMEM((count * PLANES, NG, NG), F32), pltpu.SemaphoreType.DMA((count,))],
    )


def exchanged(array):
    flat = array.reshape(-1, 128)
    return lax.all_to_all(flat, "slab", 0, 0, tiled=True).reshape(array.shape)


def moved(name, array, pairs):
    with jax.named_scope(name):
        return lax.ppermute(array, "band", pairs)


def shards(orbitals):
    t = {name: jnp.asarray(table) for name, table in tables().items()}
    bands = lax.axis_size("band")
    core = lax.rem(lax.axis_index("band"), 2).astype(jnp.int32).reshape(1)
    slab = lax.axis_index("slab").astype(jnp.int32).reshape(1)
    outward = [(g, (g - 2) % bands if g % 2 == 0 else (g + 2) % bands) for g in range(bands)]
    homeward = [(b, a) for a, b in outward]
    across = [(g, g ^ 1) for g in range(bands)]

    groups = range(len(GROUPS))
    own = [packed(orbitals, g) for g in groups]
    vis = [moved(f"visit_{g}", own[g], outward) for g in groups]
    swap = [moved(f"swap_{g}", own[g], across) for g in groups]

    fields, befores, state = [], [], None
    for g in groups:
        if g == 1:
            swap[2], *state = lax.optimization_barrier((fetched(swap[2]), *state))
        befores.append(state and state[0])
        field, state = transformed(g, core, own[g], swap[g], vis[g], state, t)
        fields.append(field)
    state, slab, core, mine = lax.optimization_barrier((state, slab, core, picked(slab, t)))
    coming, mean = solved(slab, exchanged(state), mine, t)
    coming = exchanged(coming)

    def at_group(g, state):
        return products(g, core, own[g], swap[g], vis[g], fields[g], befores[g], coming, mean, state, t)

    def home(g, part):
        return moved(f"return_{g}", part, homeward)

    def cross(g, part):
        return moved(f"cross_{g}", part, across)

    sent, partner_2, kept_2, state = at_group(2, None)
    returned_2 = home(2, sent)
    sent, partner, kept_1, state = at_group(1, state)
    partner_2, partner = lax.optimization_barrier((partner_2, partner))
    returned_1 = home(1, sent)
    crossed_2, crossed_1 = cross(2, partner_2), cross(1, partner)
    returned_2, *state = lax.optimization_barrier((returned_2, *state))
    sent, partner, kept_0, state = at_group(0, state)
    returned_0, crossed_0 = home(0, sent), cross(0, partner)
    result = finished(2, kept_2, crossed_2, returned_2, None)
    result = finished(1, kept_1, crossed_1, returned_1, result)
    return finished(0, kept_0, crossed_0, returned_0, result)


def solution(mesh):
    spec = P("band", "slab", None, None)
    return jax.shard_map(shards, mesh=mesh, in_specs=(spec,), out_specs=spec, check_vma=False)
```

```python
import functools

import jax
import jax.numpy as jnp
import ml_dtypes
import numpy as np
from jax import lax
from jax.experimental import pallas as pl
from jax.experimental.pallas import tpu as pltpu
from jax.sharding import PartitionSpec as P

NG = 160
SLABS = 8
DEPTH = NG // SLABS
PLANES = 4
CHUNKS = DEPTH // PLANES
WIDE = 256
MODE_TILES = NG * NG // 1024
SEND_TILES = 13
F32 = jnp.float32
BF16 = jnp.bfloat16


def split_table(table):
    high = table.astype(np.float32).astype(ml_dtypes.bfloat16)
    low = (table - high.astype(np.float64)).astype(np.float32).astype(ml_dtypes.bfloat16)
    return high, low


def stacked(table, axis):
    high, low = split_table(table)
    return np.concatenate([high, high, low] if axis == 0 else [high, low, high], axis=axis)


def plane_tiles(plane):
    main = plane[:, :128].reshape(-1, 8, 128)
    rest = np.concatenate([plane[40 * g : 40 * g + 40, 128:] for g in range(4)], axis=1)
    return np.concatenate([main, rest.reshape(-1, 8, 128)])


def widened(plane):
    return np.pad(plane, [(0, 0)] * (plane.ndim - 1) + [(0, WIDE - NG)])


@functools.cache
def tables():
    index = np.arange(NG)
    angle = 2.0 * np.pi * (index[:, None] * index[None, :] % NG) / NG
    hartley = np.cos(angle) + np.sin(angle)
    forward = np.zeros((WIDE, WIDE))
    forward[:128, :NG] = hartley[:128]
    forward[128:, :NG] = np.tile(hartley[128:], (PLANES, 1))
    inverse = np.zeros((WIDE, WIDE))
    inverse[:NG, :128] = hartley[:, :128]
    inverse[:NG, 128:] = np.tile(hartley[:, 128:], (1, PLANES))
    wave = 4.0 * np.sin(np.pi * index / NG) ** 2
    lam = wave[:, None] + wave[None, :]
    ratio = 1.0 / (1.0 + lam / 2 + np.sqrt(lam + lam * lam / 4))
    ratio[0, 0] = 0.0
    scale = ratio / (1.0 - ratio**2) / NG**2
    powers = np.stack([ratio ** (PLANES * k) for k in range(CHUNKS)])
    edge = np.stack([scale * ratio ** (i + 1) for i in range(DEPTH)])
    jump = np.tile(plane_tiles(ratio**DEPTH), (4, 1, 1))
    wrap = np.tile(plane_tiles(1.0 / (1.0 - ratio**NG)), (4, 1, 1))
    spare = [(0, SLABS * SEND_TILES - 4 * MODE_TILES), (0, 0), (0, 0)]
    zero = np.zeros((SLABS, 24, 128))
    for apart in range(SLABS):
        for i in range(DEPTH):
            d = (DEPTH * apart + i - np.arange(DEPTH)) % NG
            zero[apart, i, :DEPTH] = ((NG**2 - 1) / (12 * NG) - d * (NG - d) / (2 * NG)) / NG**2
    as32 = lambda a: a.astype(np.float32)
    return dict(
        forward=stacked(forward, 0),
        inverse=stacked(inverse, 0),
        hartley=stacked(hartley, 1),
        ratio=as32(widened(ratio)),
        scale=as32(widened(scale)),
        powers=as32(widened(powers)),
        edge=as32(widened(edge)),
        jump=as32(np.pad(jump, spare)),
        wrap=as32(np.pad(wrap, spare)),
        zero=as32(zero),
    )


def split(value):
    high = value.astype(BF16)
    return high, (value - high.astype(F32)).astype(BF16)


def dot(a, b):
    return jnp.dot(a, b, preferred_element_type=F32)


def times_table(value, table):
    high, low = split(value)
    return dot(jnp.concatenate([high, low, high], axis=1), table)


def table_times(table, value):
    high, low = split(value)
    return dot(table, jnp.concatenate([high, high, low], axis=0))


VMEM = pl.BlockSpec(memory_space=pltpu.VMEM)
SMEM = pl.BlockSpec(memory_space=pltpu.SMEM)
HBM = pl.BlockSpec(memory_space=pltpu.HBM)
GROUPS = (2, 2, 1)
FIRST = tuple(sum(GROUPS[:g]) for g in range(len(GROUPS)))


def call(kernel, name, operands, outs, in_specs=None, out_specs=VMEM, limit=14, **kwargs):
    if in_specs is None:
        in_specs = [VMEM] * len(operands)
    return pl.pallas_call(
        kernel,
        name=name,
        out_shape=outs,
        in_specs=in_specs,
        out_specs=jax.tree.map(lambda a: out_specs, outs),
        compiler_params=pltpu.CompilerParams(vmem_limit_bytes=limit * 2**20),
        cost_estimate=pl.CostEstimate(flops=1, bytes_accessed=1, transcendentals=0),
        **kwargs,
    )(*operands)


def at(g, arrays):
    place = pltpu.VMEM if g == len(GROUPS) - 1 else pltpu.HBM
    return [pltpu.with_memory_space_constraint(a, place) for a in arrays]


def kept_close(arrays):
    return [pltpu.with_memory_space_constraint(a, pltpu.VMEM) for a in arrays]


def space(g):
    return pltpu.VMEM


def resting(g):
    return pltpu.VMEM


def f32_shape(*shape):
    return jax.ShapeDtypeStruct(shape, F32)


def group_shape(g):
    return space(g)((GROUPS[g] * (PLANES + 1), NG, 128), F32)


def own_shape(g):
    return pltpu.HBM((GROUPS[g] * (PLANES + 1), NG, 128), F32) if g == 1 else group_shape(g)


def packed(orbitals, g):
    count = GROUPS[g]
    close = g != 1

    def kernel(orbitals, out, block, *refs):
        ready, (arrived, gone) = (out, refs) if close else (refs[0], refs[1:])
        comes, goes = [], []
        for z in range(count * PLANES):
            there = orbitals.at[0, FIRST[g] * PLANES + z]
            comes.append(pltpu.make_async_copy(there, block.at[z], arrived.at[z]))
            comes[z].start()
        for c in range(count):
            base = c * (PLANES + 1)
            planes = range(c * PLANES, (c + 1) * PLANES)
            for j, z in enumerate(planes):
                comes[z].wait()
                ready[base + j] = block[z, :, :128]
            ready[base + PLANES] = jnp.concatenate([block[z, :, 128:] for z in planes], axis=1)
            if not close:
                part = pl.ds(base, PLANES + 1)
                goes.append(pltpu.make_async_copy(ready.at[part], out.at[part], gone.at[c]))
                goes[c].start()
        for copy in goes:
            copy.wait()

    scratch = [pltpu.VMEM((count * PLANES, NG, NG), F32)]
    if not close:
        scratch.append(pltpu.VMEM(group_shape(g).shape, F32))
    return call(
        kernel,
        f"pack_{g}",
        [pltpu.with_memory_space_constraint(orbitals, pltpu.HBM)],
        own_shape(g),
        [HBM],
        VMEM if close else HBM,
        scratch_shapes=scratch + [pltpu.SemaphoreType.DMA((n,)) for n in (count * PLANES, count)],
    )


def fetched(array):
    def kernel(array, out, arrived):
        copy = pltpu.make_async_copy(array, out, arrived)
        copy.start()
        copy.wait()

    return call(
        kernel,
        "fetch",
        [pltpu.with_memory_space_constraint(array, pltpu.HBM)],
        pltpu.VMEM(array.shape, F32),
        [HBM],
        scratch_shapes=[pltpu.SemaphoreType.DMA],
    )


def strip():
    return lax.broadcasted_iota(jnp.int32, (NG, 128), 1) // (128 // PLANES)


def to_tiles(plane):
    rest = plane[:, 128:]
    moved = rest[:40]
    for g in range(1, 4):
        moved = moved + pltpu.roll(rest[40 * g : 40 * g + 40], 32 * g, 1)
    return plane[:, :128].reshape(-1, 8, 128), moved.reshape(-1, 8, 128)


def from_tiles(tiles):
    main = jnp.concatenate(tiles[:20], axis=0)
    rest = jnp.concatenate(tiles[20:], axis=0)
    lane = lax.broadcasted_iota(jnp.int32, rest.shape, 1)
    parts = [rest] + [pltpu.roll(rest, 128 - 32 * g, 1) for g in range(1, 4)]
    rest = jnp.concatenate([jnp.where(lane < 32, part, 0.0) for part in parts], axis=0)
    return jnp.concatenate([main, rest], axis=1)


def transformed(g, core, own, swap, vis, state, t):
    first, last = g == 0, g == len(GROUPS) - 1

    def kernel(*refs):
        core, own, swap, vis, table, hartley, ratio, powers = refs[:8]
        refs = refs[8:]
        if not first:
            right0, left0, zero0 = refs[:3]
            refs = refs[3:]
        fields, *results = refs
        second = core[0] == 1
        h, r, x_table, owner = hartley[...], ratio[...], table[...], strip()
        row = lax.broadcasted_iota(jnp.int32, (8, 128), 0)
        lane = lax.broadcasted_iota(jnp.int32, (8, 128), 1)
        means = jnp.zeros((8, 128), F32) if first else zero0[...]
        rights = [None if first else right0[pair] for pair in range(2)]
        lefts = [None if first else left0[pair] for pair in range(2)]
        for c in range(GROUPS[g]):
            start = c * (PLANES + 1)
            densities = []
            for p in range(start, start + PLANES + 1):
                other = jnp.where(second, vis[p], own[p])
                densities.append((own[p] * vis[p], other * swap[p]))
            for j in range(PLANES):
                wide = [
                    jnp.concatenate([densities[j][pair], jnp.where(owner == j, densities[PLANES][pair], 0.0)], axis=1)
                    for pair in range(2)
                ]
                along_x = times_table(jnp.concatenate(wide, axis=0), x_table)
                z = PLANES * c + j
                for pair in range(2):
                    field = table_times(h, along_x[NG * pair : NG * (pair + 1)])
                    fields[pair, z] = field
                    rights[pair] = field if rights[pair] is None else r * rights[pair] + field
                    here = (row == pair) & (lane == PLANES * FIRST[g] + z)
                    means = jnp.where(here, jnp.broadcast_to(field[:1, :1], (8, 128)), means)
            for pair in range(2):
                back = fields[pair, PLANES * c + PLANES - 1]
                for j in reversed(range(PLANES - 1)):
                    back = r * back + fields[pair, PLANES * c + j]
                lefts[pair] = back if lefts[pair] is None else lefts[pair] + powers[FIRST[g] + c] * back
        if not last:
            right, left, zero = results
            for pair in range(2):
                right[pair] = rights[pair]
                left[pair] = lefts[pair]
            zero[...] = means
            return
        (out,) = results
        for number, plane in enumerate(rights + lefts):
            main, rest = to_tiles(plane)
            for i in range(MODE_TILES):
                tile = main[i] if i < 20 else rest[i - 20]
                to, slot = divmod(MODE_TILES * number + i, SEND_TILES)
                out[to, slot] = tile
        for i in range(4 * MODE_TILES, SLABS * SEND_TILES):
            out[i // SEND_TILES, i % SEND_TILES] = jnp.zeros((8, 128), F32)
        for to in range(SLABS):
            out[to, SEND_TILES] = means

    outs = [resting(g)((2, GROUPS[g] * PLANES, NG, WIDE), F32)]
    if last:
        outs += [f32_shape(SLABS, SEND_TILES + 1, 8, 128)]
    else:
        outs += [space(g + 1)((2, NG, WIDE), F32)] * 2 + [f32_shape(8, 128)]
    operands = [core, *(at(g, [own]) if g == 1 else kept_close([own])), *at(g, [swap, vis])]
    operands += kept_close([t["forward"], t["hartley"], t["ratio"], t["powers"]])
    if not first:
        operands += [*kept_close(state[:2]), state[2]]
    field, *state = call(
        kernel, f"forward_{g}", operands, outs, [SMEM] + [VMEM] * (len(operands) - 1)
    )
    return field, (state[0] if last else state)


def picked(slab, t):
    def kernel(slab, jumps, wraps, out, arrived):
        mine = pl.ds(slab[0] * SEND_TILES, SEND_TILES)
        copies = [
            pltpu.make_async_copy(table.at[mine], out.at[i], arrived.at[i])
            for i, table in enumerate((jumps, wraps))
        ]
        for copy in copies:
            copy.start()
        for copy in copies:
            copy.wait()

    tables = [pltpu.with_memory_space_constraint(t[name], pltpu.HBM) for name in ("jump", "wrap")]
    return call(
        kernel,
        "pick",
        [slab, *tables],
        pltpu.VMEM((2, SEND_TILES, 8, 128), F32),
        [SMEM, HBM, HBM],
        scratch_shapes=[pltpu.SemaphoreType.DMA((2,))],
    )


def solved(slab, moments, tables, t):
    def kernel(slab, moments, tables, zero, out, mean):
        me = slab[0]
        for slot in range(SEND_TILES):
            leftward = me * SEND_TILES + slot >= 2 * MODE_TILES
            place = lambda p: jnp.where(leftward, SLABS - 1 - p, p)
            values = [moments[place(p), slot] for p in range(SLABS)]
            r = tables[0, slot]
            run = values[0]
            for p in range(1, SLABS):
                run = run * r + values[p]
            run = run * tables[1, slot]
            for p in range(SLABS):
                out[place(p), slot] = run
                run = values[p] + r * run
        for pair in range(2):
            total = jnp.zeros((24, 128), F32)
            for p in range(SLABS):
                apart = lax.rem(me - p + SLABS, SLABS)
                total = total + zero[apart] * moments[p, SEND_TILES, pair : pair + 1, :]
            mean[pair] = jnp.broadcast_to(jnp.sum(total, axis=1, keepdims=True), (24, 128))

    return call(
        kernel,
        "solve",
        [slab, moments, *kept_close([tables, t["zero"]])],
        [f32_shape(SLABS, SEND_TILES, 8, 128), f32_shape(2, 24, 128)],
        [SMEM, VMEM, VMEM, VMEM],
    )


def products(g, core, own, swap, vis, field, before, coming, mean, state, t):
    first, whole = state is None, before is not None

    def kernel(core, own, swap, vis, fields, mean, edge, ratio, scale, table, hartley, *refs):
        if whole:
            before = refs[0]
            refs = refs[1:]
        if first:
            tiles = [[refs[0][divmod(MODE_TILES * n + i, SEND_TILES)] for i in range(MODE_TILES)] for n in range(4)]
            edges = [from_tiles(list_) for list_ in tiles]
            refs = refs[1:]
        else:
            edges = [refs[n // 2][n % 2] for n in range(4)]
            refs = refs[2:]
        sent, crossed, kept, right, left = refs
        rights, lefts = edges[:2], edges[2:]
        second = core[0] == 1
        h, r, c, x_table, owner = hartley[...], ratio[...], scale[...], table[...], strip()
        count = GROUPS[g] * PLANES
        sums = [[], []]
        for pair in range(2):
            run = before[pair] if whole else None
            for z in range(count):
                run = fields[pair, z] if run is None else r * run + fields[pair, z]
                sums[pair].append(run)
        for k in reversed(range(GROUPS[g])):
            start = k * (PLANES + 1)
            rests = [None, None]

            def share(p, x, y):
                resident, partner, visiting = own[p], swap[p], vis[p]
                extra = y * partner
                sent[p] = x * resident + jnp.where(second, extra, 0.0)
                kept[p] = x * visiting + jnp.where(second, 0.0, extra)
                crossed[p] = y * jnp.where(second, visiting, resident)

            for j in reversed(range(PLANES)):
                z = PLANES * k + j
                along_y = []
                for pair in range(2):
                    run = r * lefts[pair]
                    value = c * (sums[pair][z] + run) + edge[z] * rights[pair]
                    lefts[pair] = run + fields[pair, z]
                    along_y.append(table_times(h, value))
                both = times_table(jnp.concatenate(along_y, axis=0), x_table)
                middles = [mean[pair, PLANES * FIRST[g] + z : PLANES * FIRST[g] + z + 1, :1] for pair in range(2)]
                parts = [both[:NG] + middles[0], both[NG:] + middles[1]]
                for pair in range(2):
                    rest = parts[pair][:, 128:]
                    rests[pair] = rest if rests[pair] is None else jnp.where(owner == j, rest, rests[pair])
                share(start + j, parts[0][:, :128], parts[1][:, :128])
            share(start + PLANES, *rests)
        for pair in range(2):
            right[pair] = rights[pair]
            left[pair] = lefts[pair]

    count = GROUPS[g] * PLANES
    edge = t["edge"][PLANES * FIRST[g] : PLANES * FIRST[g] + count]
    operands = [core, *(at(g, [own]) if g == 1 else kept_close([own])), *at(g, [swap, vis]), *kept_close([field]), mean]
    operands += kept_close([edge, t["ratio"], t["scale"], t["inverse"], t["hartley"]])
    if whole:
        operands += kept_close([before])
    operands += [coming] if first else kept_close(state)
    planes = space(g)((2, NG, WIDE), F32)
    sent, crossed, kept, *state = call(
        kernel,
        f"products_{g}",
        operands,
        [group_shape(g)] * 3 + [planes] * 2,
        [SMEM] + [VMEM] * (len(operands) - 1),
    )
    return sent, crossed, kept, state


def finished(g, kept, crossed, returned, result):
    count = GROUPS[g]

    def kernel(kept, crossed, returned, *refs):
        out, block, gone = refs[-3:]
        copies = []
        for c in range(count):
            base = c * (PLANES + 1)
            rest = kept[base + PLANES] + crossed[base + PLANES] + returned[base + PLANES]
            for j in range(PLANES):
                z = c * PLANES + j
                block[z, :, :128] = kept[base + j] + crossed[base + j] + returned[base + j]
                moved = rest if j == 0 else pltpu.roll(rest, 128 - 32 * j, 1)
                block[z, :, 128:] = moved[:, :32]
            here = pl.ds(c * PLANES, PLANES)
            there = pl.ds((FIRST[g] + c) * PLANES, PLANES)
            copies.append(pltpu.make_async_copy(block.at[here], out.at[0, there], gone.at[c]))
            copies[c].start()
        for copy in copies:
            copy.wait()

    operands = [kept, crossed, returned]
    specs = [VMEM] * 3
    aliases = {}
    if result is not None:
        operands.append(result)
        specs.append(HBM)
        aliases = {3: 0}
    return call(
        kernel,
        f"finish_{g}",
        operands,
        pltpu.HBM((1, DEPTH, NG, NG), F32),
        specs,
        HBM,
        input_output_aliases=aliases,
        scratch_shapes=[pltpu.VMEM((count * PLANES, NG, NG), F32), pltpu.SemaphoreType.DMA((count,))],
    )


def exchanged(array):
    flat = array.reshape(-1, 128)
    return lax.all_to_all(flat, "slab", 0, 0, tiled=True).reshape(array.shape)


def moved(name, array, pairs):
    with jax.named_scope(name):
        return lax.ppermute(array, "band", pairs)


def shards(orbitals):
    t = {name: jnp.asarray(table) for name, table in tables().items()}
    bands = lax.axis_size("band")
    core = lax.rem(lax.axis_index("band"), 2).astype(jnp.int32).reshape(1)
    slab = lax.axis_index("slab").astype(jnp.int32).reshape(1)
    outward = [(g, (g - 2) % bands if g % 2 == 0 else (g + 2) % bands) for g in range(bands)]
    homeward = [(b, a) for a, b in outward]
    across = [(g, g ^ 1) for g in range(bands)]

    groups = range(len(GROUPS))
    own = [packed(orbitals, g) for g in groups]
    vis = [moved(f"visit_{g}", own[g], outward) for g in groups]
    swap = [moved(f"swap_{g}", own[g], across) for g in groups]

    fields, befores, state = [], [], None
    for g in groups:
        if g == 1:
            swap[2], *state = lax.optimization_barrier((fetched(swap[2]), *state))
        befores.append(state and state[0])
        field, state = transformed(g, core, own[g], swap[g], vis[g], state, t)
        fields.append(field)
    state, slab, core, mine = lax.optimization_barrier((state, slab, core, picked(slab, t)))
    coming, mean = solved(slab, exchanged(state), mine, t)
    coming = exchanged(coming)

    def at_group(g, state):
        return products(g, core, own[g], swap[g], vis[g], fields[g], befores[g], coming, mean, state, t)

    def home(g, part):
        return moved(f"return_{g}", part, homeward)

    def cross(g, part):
        return moved(f"cross_{g}", part, across)

    sent, partner_2, kept_2, state = at_group(2, None)
    returned_2 = home(2, sent)
    sent, partner, kept_1, state = at_group(1, state)
    partner_2, partner = lax.optimization_barrier((partner_2, partner))
    returned_1 = home(1, sent)
    crossed_2, crossed_1 = cross(2, partner_2), cross(1, partner)
    returned_2, *state = lax.optimization_barrier((returned_2, *state))
    sent, partner, kept_0, state = at_group(0, state)
    returned_0, crossed_0 = home(0, sent), cross(0, partner)
    result = finished(2, kept_2, crossed_2, returned_2, None)
    result = finished(1, kept_1, crossed_1, returned_1, result)
    return finished(0, kept_0, crossed_0, returned_0, result)


def solution(mesh):
    spec = P("band", "slab", None, None)
    return jax.shard_map(shards, mesh=mesh, in_specs=(spec,), out_specs=spec, check_vma=False)
```
